512 devices in a mesh: pop: 64 (over z, x_lo, core), tensor: 8 (over y, x_hi).
Axes of the slice: x: 4 (x_hi: 2, x_lo: 2; x = x_hi * 2 + x_lo), y: 4, z: 16, core: 2. Of those that a mesh axis runs over, the one named last changes fastest.
Arguments:
- tokens: bfloat16 [12288, 5120], P('pop', 'tensor'), may hold values from -6 to 6
- base_weight: float32 [5120, 5120], P('tensor', 'pop'), may hold values from -0.078125 to 0.078125
- left_factors: float32 [512, 4, 5120], P('pop', None, 'tensor'), may hold values from -0.078125 to 0.078125
- right_factors: float32 [512, 4, 5120], P('pop'), may hold values from -6 to 6
- member_of: int32 [64, 192], P('pop'), may hold values from 0 to 7, never falling along the last dimension, each value on 1 to 96 neighbouring positions
- ranks: int32 [512], P('pop'), may hold values from 0 to 63
Outputs:
- outputs: float32 [12288, 5120], P('pop', 'tensor')
- update: float32 [5120, 5120], P('tensor', 'pop')
The draws below stay inside these ranges and needn't reach their ends.
Inputs may be any that keep to these rules, and one draw needn't show every extreme that they name: A row g * 192 + r belongs to member g * 8 + member_of[g, r]; within each g the values never fall, every member has 1 to 96 rows and one has exactly 96.
All inputs are finite; a program needn't handle non-finite values.
Results may differ from the reference program's by a relative error of at most 0.0026.
Values may be sent and summed in bfloat16 or wider, within the bound.
No kernel may reach another device: no remote copies, remote signals or barrier semaphores. Data moves between devices by JAX's collectives and lax.ppermute only.
A program may use at most 128 MiB of HBM per device.

```python
import math
import jax
import jax.numpy as jnp
import numpy as np
from jax import lax

D = 5120
RANK = 4
M_DEV = 8
ROWS_DEV = 192
RANK_MAX = 64
GROUPS = 64
MEMBERS = 512
ROWS = 12288


def draw_ranks(key, part):
    key = jax.random.fold_in(key, 11)
    groups = MEMBERS // M_DEV
    last_index = max(groups - 1, 1)
    position = jnp.arange(MEMBERS, dtype=jnp.int32) // M_DEV
    ceiling = RANK_MAX * (last_index + 2 * position) // (3 * last_index)
    raw_bits = jax.random.randint(key, (MEMBERS,), 0, 1 << 20, dtype=jnp.int32)
    values = raw_bits % jnp.maximum(ceiling, 1)
    values = values.at[0].set(0).at[MEMBERS - M_DEV].set(RANK_MAX - 1)
    return values.astype(jnp.int32)


def steps_of(stream_key, extent, split, low, top_value):
    level = 1.0
    for dim, parts in split:
        draws = jax.random.uniform(jax.random.fold_in(jax.random.fold_in(stream_key, 6), dim), (parts,), jnp.float32, low / len(split), top_value / len(split))
        level = level * jnp.repeat(jnp.exp(draws), extent[dim] // parts).reshape((-1,) + (1,) * (len(extent) - 1 - dim))
    return level


def profile(number_of, total, limit, lean):
    portions = [(1 << 20) // math.isqrt(grade ** lean) + 1 for grade in range(2, number_of + 1)]
    spare, counts = total - limit - (number_of - 1), [1] * (number_of - 1)
    while spare > 0:
        free = [i for i in range(number_of - 1) if counts[i] < limit]
        whole, budget = sum([portions[i] for i in free]), spare
        for i in free:
            addition = min(limit - counts[i], max(1, budget * portions[i] // whole), spare)
            counts[i] = counts[i] + addition
            spare = spare - addition
    return np.array([limit] + counts)


def ragged_sizes(own_key, amount, total, reach, slope):
    if amount == 2:
        one = jax.random.randint(own_key, (), max(1, total - reach), min(reach, total - 1) + 1)
        return jnp.stack([one, total - one])
    sizes = jnp.asarray(profile(amount, total, reach, slope), jnp.int32)
    twos = (amount - 1) // 2
    giver, sink = sizes[1:1 + 2 * twos:2], sizes[2:2 + 2 * twos:2]
    room = jnp.minimum(giver - 1, reach - sink)
    passed = jax.random.randint(jax.random.fold_in(own_key, 1), (twos,), 0, 1 << 20) % (room + 1)
    sizes = sizes.at[1:1 + 2 * twos:2].set(giver - passed).at[2:2 + 2 * twos:2].set(sink + passed)
    return sizes[jax.random.permutation(jax.random.fold_in(own_key, 2), amount)]


def gaussian(own_key, shape, spread, most, split=(), held_as=jnp.bfloat16):
    drawn = jax.random.normal(own_key, shape, jnp.float32) * spread
    if len(split) > 0:
        drawn = steps_of(own_key, shape, split, -0.22, 0.18) * drawn
    return jnp.clip(drawn, min=-most, max=most).astype(held_as)


def setup_inputs(seed: int = 0) -> dict:
    streams_of = jax.random.split(jax.random.key(seed), 7)
    return {
        "tokens": gaussian(streams_of[0], (ROWS, D), 1.0, 6.0, ((0, 64), (1, 8))),
        "base_weight": gaussian(streams_of[1], (D, D), D ** -0.5, 0.078125, ((0, 8), (1, 64)), jnp.float32),
        "left_factors": gaussian(streams_of[2], (MEMBERS, RANK, D), D ** -0.5, 0.078125, ((0, 64), (2, 8)), jnp.float32),
        "right_factors": gaussian(streams_of[3], (MEMBERS, RANK, D), 1.0, 6.0, ((0, 64),), jnp.float32),
        "member_of": jax.vmap(lambda own: jnp.searchsorted(jnp.cumsum(ragged_sizes(own, M_DEV, ROWS_DEV, ROWS_DEV // 2, 1)), jnp.arange(ROWS_DEV), side="right"))(jax.random.split(streams_of[4], GROUPS)).reshape((GROUPS, ROWS_DEV)).astype(jnp.int32),
        "ranks": draw_ranks(jax.random.fold_in(streams_of[6], 71), 0),
    }


perturb_scale = 0.5

def reference(tokens, base_weight, left_factors, right_factors, member_of, ranks):
    groups = member_of.shape[0]
    base_half = base_weight.astype(jnp.bfloat16)
    base_out = jnp.dot(tokens, base_half, preferred_element_type=jnp.float32)
    token_float = tokens.astype(jnp.float32).reshape(groups, ROWS_DEV, D)
    left_groups = left_factors.reshape(groups, M_DEV, RANK, D)
    right_groups = right_factors.reshape(groups, M_DEV, RANK, D)

    def one_group(items):
        row_block, member_ids, left_block, right_block = items
        selector = (member_ids[:, None] == jnp.arange(M_DEV, dtype=jnp.int32)[None, :]).astype(jnp.float32)
        projected = jnp.einsum('rd,mkd->mkr', row_block, left_block, precision=lax.Precision.HIGHEST)
        coefficient = lax.optimization_barrier(jnp.sum(projected * selector.T[:, None, :], axis=0))
        weighted = coefficient[None, :, :] * selector.T[:, None, :]
        return jnp.einsum('mkr,mkd->rd', weighted, right_block, precision=lax.Precision.HIGHEST)
    low_rank = lax.map(one_group, (token_float, member_of, left_groups, right_groups)).reshape(ROWS, D)
    outputs = base_out + perturb_scale / math.sqrt(RANK) * low_rank
    rank_values = ranks.astype(jnp.float32)
    rank_mean = jnp.mean(rank_values)
    variance = jnp.mean((rank_values - rank_mean) ** 2)
    fitness = (rank_values - rank_mean) / jnp.sqrt(variance + 1e-05)
    weighted_left = (fitness[:, None, None] * left_factors).reshape(MEMBERS * RANK, D)
    update_scale = math.sqrt(D / (MEMBERS * RANK))
    update = update_scale * jnp.einsum('ni,nj->ij', weighted_left, right_factors.reshape(MEMBERS * RANK, D), precision=lax.Precision.HIGHEST)
    return (outputs, update)
```

```python
import functools
import itertools
import math

import jax
import jax.numpy as jnp
from jax import lax
from jax.experimental import pallas as pl
from jax.experimental.pallas import tpu as pltpu
from jax.sharding import Mesh
from jax.sharding import PartitionSpec as P

D = 5120
RANK = 4
M_DEV = 8
ROWS = 192
IN_BLOCK = 640
OUT_BLOCK = 80
EXTRA = 112

perturb_scale = 0.5

SIZES = {"z": 16, "xl": 2, "core": 2, "y": 4, "xh": 2}
AXES = tuple(SIZES)
POP = ("z", "xl", "core")
TENSOR = ("y", "xh")
BF16 = jnp.bfloat16
F32 = jnp.float32


def flat(place):
    index = 0
    for value, size in zip(place, SIZES.values()):
        index = index * size + value % size
    return index


def move(value, target):
    places = itertools.product(*(range(n) for n in SIZES.values()))
    return lax.ppermute(value, AXES, [(flat(p), flat(target(*p))) for p in places])


def weight_target(shift, z, xl, core, y, xh):
    owner = z // 2
    to_y, to_xh = owner // 2, owner % 2
    column = (z % 2) * 4 + xl * 2 + core
    near = (y - to_y) % 4
    return ((near // 2) * 8 + column + shift, xh, near % 2, to_y, to_xh)


def right_target(flip, z, xl, core, y, xh):
    half = z // 2
    return (2 * (2 * y + xh) + ((z % 2) ^ flip), half // 4, core, half % 4, xl)


def rows_target(flip, z, xl, core, y, xh):
    return (z, xh, core, y, xl ^ flip)


def ring_target(z, xl, core, y, xh):
    return (z + (1 if core == 0 else -1), xl, core, y, xh)


def core_target(z, xl, core, y, xh):
    return (z, xl, 1 - core, y, xh)


def xl_target(z, xl, core, y, xh):
    return (z, 1 - xl, core, y, xh)


def y_target(step, z, xl, core, y, xh):
    return (z, xl, core, y + step, xh)


def y_far_target(z, xl, core, y, xh):
    return (z, xl, core, y + (1 if core == 0 else -1), xh)


def nt_dot(a, b):
    return lax.dot_general(a, b, (((1,), (1,)), ((), ())), preferred_element_type=F32)


def split(value):
    high = lax.reduce_precision(value, 8, 7)
    return high.astype(BF16), (value - high).astype(BF16)


def product_kernel(
    place, q, r1, r2, r3, s1, s2, s3, r4, s4, t0, t1, t2, t3, mine, mine_proj, give, weights, total, proj
):
    z, core, own = place[0], place[1], place[2]
    sign = 2 * core - 1

    def put(near, column, block):
        rows = pl.ds(pl.multiple_of(column * OUT_BLOCK, 16), OUT_BLOCK)
        weights[near, rows, :] = block

    def put_all(offset, ref):
        column = lax.rem(z + 16 + offset, 8)
        for near in range(4):
            put(near, column, ref[near * OUT_BLOCK : (near + 1) * OUT_BLOCK, :])

    put_all(0, q)
    for step, (ring, swapped) in enumerate(((r1, s1), (r2, s2), (r3, s3)), 1):
        put_all(sign * step, ring)
        put_all(-sign * step, swapped)
    last = lax.rem(z + 4, 8)
    for i in range(2):
        put(2 * core + i, last, r4[i * OUT_BLOCK : (i + 1) * OUT_BLOCK, :])
        put(2 * (1 - core) + i, last, s4[i * OUT_BLOCK : (i + 1) * OUT_BLOCK, :])

    for near, rows in enumerate((t0, t1, t2, t3)):
        part = nt_dot(rows[: 2 * ROWS, :], weights[near])
        total[...] = part if near == 0 else total[...] + part
        for m in range(2):
            left = rows[2 * ROWS + m * EXTRA : 2 * ROWS + m * EXTRA + 32, :]
            part = nt_dot(rows[m * ROWS : (m + 1) * ROWS, :], left)
            block = slice(m * ROWS, (m + 1) * ROWS)
            proj[block, :] = part if near == 0 else proj[block, :] + part
    here = pl.ds(pl.multiple_of(own * ROWS, ROWS), ROWS)
    there = pl.ds(pl.multiple_of((1 - own) * ROWS, ROWS), ROWS)
    mine[...] = total[here, :]
    mine_proj[...] = proj[here, :]
    give[:, :IN_BLOCK] = total[there, :].astype(BF16)
    give[:, IN_BLOCK:] = jnp.zeros((ROWS, 256), BF16)
    high = proj[there, :].astype(BF16)
    give[:, IN_BLOCK : IN_BLOCK + 32] = high
    give[:, IN_BLOCK + 128 : IN_BLOCK + 160] = (proj[there, :] - high.astype(F32)).astype(BF16)


def product(place, *arrays):
    vmem = pl.BlockSpec(memory_space=pltpu.VMEM)
    return pl.pallas_call(
        product_kernel,
        out_shape=(
            jax.ShapeDtypeStruct((ROWS, IN_BLOCK), F32),
            jax.ShapeDtypeStruct((ROWS, 32), F32),
            jax.ShapeDtypeStruct((ROWS, IN_BLOCK + 256), BF16),
        ),
        in_specs=[pl.BlockSpec(memory_space=pltpu.SMEM)] + [vmem] * len(arrays),
        out_specs=(vmem, vmem, vmem),
        scratch_shapes=[
            pltpu.VMEM((4, IN_BLOCK, IN_BLOCK), BF16),
            pltpu.VMEM((2 * ROWS, IN_BLOCK), F32),
            pltpu.VMEM((2 * ROWS, 32), F32),
        ],
        compiler_params=pltpu.CompilerParams(vmem_limit_bytes=40 * 2**20),
        cost_estimate=pl.CostEstimate(
            flops=2 * 384 * 640 * 2560, bytes_accessed=8 * 2**20, transcendentals=0
        ),
    )(place, *arrays)


def spread_weights(base_weight, z, core):
    piece = base_weight.T.astype(BF16)
    first = move(piece, functools.partial(weight_target, 0))
    second = move(piece, functools.partial(weight_target, 8))
    pair = jnp.where(z < 8, jnp.stack([first, second]), jnp.stack([second, first]))
    other = move(pair, core_target)
    whole = jnp.where(core == 0, jnp.stack([pair, other], 1), jnp.stack([other, pair], 1))
    return whole.reshape(4 * OUT_BLOCK, IN_BLOCK)


def ring(whole, core):
    held, swapped = [], []
    block = whole
    for step in range(4):
        if step == 3:
            half = 2 * OUT_BLOCK
            block = jnp.where(core == 0, block[:half], block[half:])
        block = move(block, ring_target)
        held.append(block)
        swapped.append(move(block, core_target))
    return held, swapped


def spread_right(right_local, ranks, z):
    chunks = right_local.reshape(32, 2, 320)
    levels = jnp.zeros((16, 320), BF16).at[0, :M_DEV].set(ranks.astype(BF16))
    parity = z % 2
    parts = []
    for flip in range(2):
        chunk = jnp.where(parity == flip, chunks[:, 0], chunks[:, 1])
        high, low = split(chunk)
        sent = jnp.concatenate([high, low, levels])
        parts.append(move(sent, functools.partial(right_target, flip)))
    return jnp.concatenate(parts, 1)


def spread_rows(payload, core):
    a = move(payload, functools.partial(rows_target, 0))
    b = move(payload, functools.partial(rows_target, 1))
    near = jnp.concatenate([a[:ROWS], b[:ROWS], a[ROWS:], b[ROWS:]])
    above = move(near, functools.partial(y_target, -1))
    below = move(near, functools.partial(y_target, 1))
    far = move(jnp.where(core == 0, below, above), y_far_target)
    return near, above, far, below


def scaled_right(blocks, z, y, xh, members):
    extra = jnp.stack([b[2 * ROWS :].reshape(2, EXTRA, 2, 320) for b in blocks])
    high, low, levels = extra[:, :, 32:64], extra[:, :, 64:96], extra[:, :, 96, :, :M_DEV]
    right = (high.astype(F32) + low.astype(F32)).transpose(0, 1, 3, 2, 4)
    levels = levels.astype(F32)
    own = jnp.pad(levels.reshape(16, M_DEV), ((0, 0), (0, 120)))
    core_side = move(own, core_target)
    both = jnp.concatenate([own[:, :M_DEV], core_side[:, :M_DEV]], 1)
    xl_side = move(jnp.pad(both, ((0, 0), (0, 112))), xl_target)
    every = jnp.concatenate([both, xl_side[:, : 2 * M_DEV]], 1)
    rank_mean = jnp.sum(every) / members
    variance = jnp.sum((every - rank_mean) ** 2) / members
    fitness = (levels - rank_mean) * lax.rsqrt(variance + 1e-05)
    scaled = jnp.repeat(fitness, RANK, axis=3)[..., None] * right
    scaled = jnp.where(xh == 0, scaled, scaled[:, ::-1])
    scaled = jnp.where(z % 2 == 0, scaled, scaled[:, :, ::-1])
    scaled = lax.dynamic_slice_in_dim(jnp.concatenate([scaled, scaled]), 4 - y, 4, 0)
    scaled = scaled.transpose(1, 0, 2, 3, 4).reshape(16 * 32, 320)
    return jnp.concatenate(split(scaled), 1)


def update_block(left_all, scaled, xl, core, members):
    product_t = lax.dot_general(
        scaled, left_all, (((0,), (0,)), ((), ())), preferred_element_type=F32
    )
    product_t = (product_t[:320] + product_t[320:]).reshape(2, 2, OUT_BLOCK, IN_BLOCK)
    keep = jnp.where(core == 0, product_t[:, 0], product_t[:, 1])
    give = jnp.where(core == 0, product_t[:, 1], product_t[:, 0])
    keep = keep + move(give, core_target)
    give = jnp.where(xl == 0, keep[1], keep[0])
    keep = jnp.where(xl == 0, keep[0], keep[1])
    total = keep + move(give, xl_target)
    return (math.sqrt(D / (members * RANK)) * total).T


def on_device(tokens, base_weight, left_factors, right_factors, member_of, ranks):
    z, xl, core, y, xh = (lax.axis_index(name) for name in AXES)
    members = M_DEV * 64
    left = left_factors.astype(BF16).reshape(32, IN_BLOCK)
    left_all = lax.all_gather(left, "z", axis=0, tiled=True)

    offset = (y * 2 + xh) * IN_BLOCK
    right_local = lax.dynamic_slice_in_dim(right_factors, offset, IN_BLOCK, 2).reshape(32, IN_BLOCK)
    whole = spread_weights(base_weight, z, core)
    right = spread_right(right_local, ranks, z)
    held, swapped = ring(whole, core)
    blocks = spread_rows(jnp.concatenate([tokens, left, right]), core)

    place = jnp.stack([z, core, xl ^ xh]).astype(jnp.int32)
    mine, mine_proj, give = product(
        place, whole, *held[:3], *swapped[:3], held[3], swapped[3], *blocks
    )
    got = move(give, xl_target).astype(F32)
    proj = mine_proj + got[:, IN_BLOCK : IN_BLOCK + 32] + got[:, IN_BLOCK + 128 : IN_BLOCK + 160]
    factor = jnp.arange(32, dtype=jnp.int32) // RANK
    mask = member_of[0][:, None] == factor[None, :]
    coefficient = jnp.where(mask, proj, 0.0) * (perturb_scale / math.sqrt(RANK))
    low_rank = jnp.dot(coefficient, right_local, precision=lax.Precision.HIGHEST)
    outputs = mine + got[:, :IN_BLOCK] + low_rank

    scaled = scaled_right(blocks, z, y, xh, members)
    update = update_block(left_all, scaled, xl, core, members)
    return (outputs, update)


def solution(mesh):
    fine = Mesh(mesh.devices.reshape(tuple(SIZES.values())), AXES)
    return jax.shard_map(
        on_device,
        mesh=fine,
        in_specs=(
            P(POP, TENSOR),
            P(TENSOR, POP),
            P(POP, None, TENSOR),
            P(POP, None, None),
            P(POP, None),
            P(POP),
        ),
        out_specs=(P(POP, TENSOR), P(TENSOR, POP)),
        check_vma=False,
    )
```

```python
import functools
import itertools
import math

import jax
import jax.numpy as jnp
from jax import lax
from jax.experimental import pallas as pl
from jax.experimental.pallas import tpu as pltpu
from jax.sharding import Mesh
from jax.sharding import PartitionSpec as P

D = 5120
RANK = 4
M_DEV = 8
ROWS = 192
IN_BLOCK = 640
OUT_BLOCK = 80
EXTRA = 64

perturb_scale = 0.5

SIZES = {"z": 16, "xl": 2, "core": 2, "y": 4, "xh": 2}
AXES = tuple(SIZES)
POP = ("z", "xl", "core")
TENSOR = ("y", "xh")
BF16 = jnp.bfloat16
F32 = jnp.float32


def flat(place):
    index = 0
    for value, size in zip(place, SIZES.values()):
        index = index * size + value % size
    return index


def move(value, target):
    places = itertools.product(*(range(n) for n in SIZES.values()))
    return lax.ppermute(value, AXES, [(flat(p), flat(target(*p))) for p in places])


def weight_target(shift, z, xl, core, y, xh):
    owner = z // 2
    to_y, to_xh = owner // 2, owner % 2
    column = (z % 2) * 4 + xl * 2 + core
    near = (y - to_y) % 4
    return ((near // 2) * 8 + column + shift, xh, near % 2, to_y, to_xh)


def right_target(flip, z, xl, core, y, xh):
    half = z // 2
    return (2 * (2 * y + xh) + ((z % 2) ^ flip), half // 4, core, half % 4, xl)


def rows_target(flip, z, xl, core, y, xh):
    return (z, xh, core, y, xl ^ flip)


def ring_target(z, xl, core, y, xh):
    return (z + (1 if core == 0 else -1), xl, core, y, xh)


def core_target(z, xl, core, y, xh):
    return (z, xl, 1 - core, y, xh)


def xl_target(z, xl, core, y, xh):
    return (z, 1 - xl, core, y, xh)


def y_target(step, z, xl, core, y, xh):
    return (z, xl, core, y + step, xh)


def y_far_target(z, xl, core, y, xh):
    return (z, xl, core, y + (1 if core == 0 else -1), xh)


def nt_dot(a, b):
    return lax.dot_general(a, b, (((1,), (1,)), ((), ())), preferred_element_type=F32)


def split(value):
    high = lax.reduce_precision(value, 8, 7)
    return high.astype(BF16), (value - high).astype(BF16)


def product_kernel(
    place, q, r1, r2, r3, s1, s2, s3, r4, s4, t0, t1, t2, t3, mine, mine_proj, give, weights, total, proj
):
    z, core, own = place[0], place[1], place[2]
    sign = 2 * core - 1

    def put(near, column, block):
        rows = pl.ds(pl.multiple_of(column * OUT_BLOCK, 16), OUT_BLOCK)
        weights[near, rows, :] = block

    def put_all(offset, ref):
        column = lax.rem(z + 16 + offset, 8)
        for near in range(4):
            put(near, column, ref[near * OUT_BLOCK : (near + 1) * OUT_BLOCK, :])

    put_all(0, q)
    for step, (ring, swapped) in enumerate(((r1, s1), (r2, s2), (r3, s3)), 1):
        put_all(sign * step, ring)
        put_all(-sign * step, swapped)
    last = lax.rem(z + 4, 8)
    for i in range(2):
        put(2 * core + i, last, r4[i * OUT_BLOCK : (i + 1) * OUT_BLOCK, :])
        put(2 * (1 - core) + i, last, s4[i * OUT_BLOCK : (i + 1) * OUT_BLOCK, :])

    for near, rows in enumerate((t0, t1, t2, t3)):
        part = nt_dot(rows[: 2 * ROWS, :], weights[near])
        total[...] = part if near == 0 else total[...] + part
        for m in range(2):
            left = rows[2 * ROWS + m * EXTRA : 2 * ROWS + m * EXTRA + 32, :]
            part = nt_dot(rows[m * ROWS : (m + 1) * ROWS, :], left)
            block = slice(m * ROWS, (m + 1) * ROWS)
            proj[block, :] = part if near == 0 else proj[block, :] + part
    here = pl.ds(pl.multiple_of(own * ROWS, ROWS), ROWS)
    there = pl.ds(pl.multiple_of((1 - own) * ROWS, ROWS), ROWS)
    mine[...] = total[here, :]
    mine_proj[...] = proj[here, :]
    give[:, :IN_BLOCK] = total[there, :].astype(BF16)
    give[:, IN_BLOCK:] = jnp.zeros((ROWS, 256), BF16)
    high = proj[there, :].astype(BF16)
    give[:, IN_BLOCK : IN_BLOCK + 32] = high
    give[:, IN_BLOCK + 128 : IN_BLOCK + 160] = (proj[there, :] - high.astype(F32)).astype(BF16)


def product(place, *arrays):
    vmem = pl.BlockSpec(memory_space=pltpu.VMEM)
    return pl.pallas_call(
        product_kernel,
        out_shape=(
            jax.ShapeDtypeStruct((ROWS, IN_BLOCK), F32),
            jax.ShapeDtypeStruct((ROWS, 32), F32),
            jax.ShapeDtypeStruct((ROWS, IN_BLOCK + 256), BF16),
        ),
        in_specs=[pl.BlockSpec(memory_space=pltpu.SMEM)] + [vmem] * len(arrays),
        out_specs=(vmem, vmem, vmem),
        scratch_shapes=[
            pltpu.VMEM((4, IN_BLOCK, IN_BLOCK), BF16),
            pltpu.VMEM((2 * ROWS, IN_BLOCK), F32),
            pltpu.VMEM((2 * ROWS, 32), F32),
        ],
        compiler_params=pltpu.CompilerParams(vmem_limit_bytes=40 * 2**20),
        cost_estimate=pl.CostEstimate(
            flops=2 * 384 * 640 * 2560, bytes_accessed=8 * 2**20, transcendentals=0
        ),
    )(place, *arrays)


def spread_weights(base_weight, z, core):
    piece = base_weight.T.astype(BF16)
    first = move(piece, functools.partial(weight_target, 0))
    second = move(piece, functools.partial(weight_target, 8))
    pair = jnp.where(z < 8, jnp.stack([first, second]), jnp.stack([second, first]))
    other = move(pair, core_target)
    whole = jnp.where(core == 0, jnp.stack([pair, other], 1), jnp.stack([other, pair], 1))
    return whole.reshape(4 * OUT_BLOCK, IN_BLOCK)


def ring(whole, core):
    held, swapped = [], []
    block = whole
    for step in range(4):
        if step == 3:
            half = 2 * OUT_BLOCK
            block = jnp.where(core == 0, block[:half], block[half:])
        block = move(block, ring_target)
        held.append(block)
        swapped.append(move(block, core_target))
    return held, swapped


def spread_right(right_local, z):
    parity = z % 2
    right = right_local.astype(BF16)
    parts = []
    for flip in range(2):
        chunk = jnp.where(parity == flip, right[:, :320], right[:, 320:])
        parts.append(move(chunk, functools.partial(right_target, flip)))
    return jnp.concatenate(parts, 1)


def spread_rows(payload, core):
    a = move(payload, functools.partial(rows_target, 0))
    b = move(payload, functools.partial(rows_target, 1))
    near = jnp.concatenate([a[:ROWS], b[:ROWS], a[ROWS:], b[ROWS:]])
    above = move(near, functools.partial(y_target, -1))
    below = move(near, functools.partial(y_target, 1))
    far = move(jnp.where(core == 0, below, above), y_far_target)
    return near, above, far, below


def rank_rows(ranks):
    own = jnp.pad(ranks.astype(F32)[None, :], ((0, 7), (0, 120)))
    both = jnp.concatenate([own[:, :M_DEV], move(own, core_target)[:, :M_DEV]], 1)
    both = jnp.pad(both, ((0, 0), (0, 112)))
    every = jnp.concatenate([both[:, : 2 * M_DEV], move(both, xl_target)[:, : 2 * M_DEV]], 1)
    return jnp.pad(every, ((0, 0), (0, IN_BLOCK - 4 * M_DEV)))


def update_kernel(members, place, left, t0, t1, t2, t3, keep, give, right, high, low, total):
    z, core, y, xh = place[0], place[1], place[3], place[4]
    lanes = lax.broadcasted_iota(jnp.int32, (8, 128), 1)
    rows = lax.broadcasted_iota(jnp.int32, (8, 128), 0)
    valid = jnp.logical_and(rows == 0, lanes < 4 * M_DEV)
    tiles = [left[i * 40 + 32 : i * 40 + 40, :128] for i in range(16)]
    rank_sum = tiles[0]
    for tile in tiles[1:]:
        rank_sum = rank_sum + tile
    rank_mean = jnp.sum(rank_sum) / members
    spread = jnp.zeros((8, 128), F32)
    for tile in tiles:
        spread = spread + jnp.where(valid, (tile - rank_mean) ** 2, 0.0)
    variance = jnp.full((8, 128), jnp.sum(spread) / members)
    scale = lax.rsqrt(variance + 1e-05)[:1, :1] * math.sqrt(D / (members * RANK))

    wide_lane = lax.broadcasted_iota(jnp.int32, (32, 128), 1)
    wide_member = lax.broadcasted_iota(jnp.int32, (32, 128), 0) // RANK
    for near, extra in enumerate((t0, t1, t2, t3)):
        for m in range(2):
            slot = (near * 2 + m) * 32
            right[slot : slot + 32, :] = extra[m * EXTRA + 32 : m * EXTRA + 64, :]
            pair = (xh ^ m) * 4 + lax.rem(y + near, 4)
            for flip in range(2):
                start = pl.multiple_of((2 * pair + (lax.rem(z, 2) ^ flip)) * 40, 8)
                levels = left[pl.ds(start + 32, 8), :128][:1, :]
                level = jnp.sum(
                    jnp.where(wide_lane == wide_member, levels, 0.0), axis=1, keepdims=True
                )
                scaled = left[pl.ds(start, 32), :] * ((level - rank_mean) * scale)
                part = scaled.astype(BF16)
                high[flip, slot : slot + 32, :] = part
                low[flip, slot : slot + 32, :] = (scaled - part.astype(F32)).astype(BF16)

    def tn_dot(a, b):
        return lax.dot_general(a, b, (((0,), (0,)), ((), ())), preferred_element_type=F32)

    first, second = right[:, :384], right[:, 256:]
    total[...] = (tn_dot(first, high[0]) + tn_dot(first, low[0]))[:320]
    total[...] += (tn_dot(second, high[1]) + tn_dot(second, low[1]))[64:]
    for i in range(2):
        here = pl.ds(pl.multiple_of((2 * i + core) * OUT_BLOCK, 8), OUT_BLOCK)
        there = pl.ds(pl.multiple_of((2 * i + 1 - core) * OUT_BLOCK, 8), OUT_BLOCK)
        keep[i] = total[here, :]
        give[i] = total[there, :]


def update_block(place, left_all, blocks, xl, members):
    vmem = pl.BlockSpec(memory_space=pltpu.VMEM)
    extra = pl.BlockSpec((2 * EXTRA, IN_BLOCK), lambda i: (2 * ROWS // (2 * EXTRA), 0))
    shape = jax.ShapeDtypeStruct((2, OUT_BLOCK, IN_BLOCK), F32)
    keep, give = pl.pallas_call(
        functools.partial(update_kernel, members),
        out_shape=(shape, shape),
        grid=(1,),
        in_specs=[pl.BlockSpec(memory_space=pltpu.SMEM), vmem] + [extra] * 4,
        out_specs=(vmem, vmem),
        scratch_shapes=[
            pltpu.VMEM((256, IN_BLOCK), BF16),
            pltpu.VMEM((2, 256, IN_BLOCK), BF16),
            pltpu.VMEM((2, 256, IN_BLOCK), BF16),
            pltpu.VMEM((320, IN_BLOCK), F32),
        ],
        compiler_params=pltpu.CompilerParams(vmem_limit_bytes=32 * 2**20),
        cost_estimate=pl.CostEstimate(
            flops=8 * 384 * 256 * 640, bytes_accessed=4 * 2**20, transcendentals=0
        ),
    )(place, left_all, *blocks)
    keep = keep + move(give, core_target)
    give = jnp.where(xl == 0, keep[1], keep[0])
    keep = jnp.where(xl == 0, keep[0], keep[1])
    return (keep + move(give, xl_target)).T


def output_kernel(scale, mine, mine_proj, got, right, member, out):
    proj = mine_proj[...]
    proj += got[:, IN_BLOCK : IN_BLOCK + 32].astype(F32)
    proj += got[:, IN_BLOCK + 128 : IN_BLOCK + 160].astype(F32)
    factor = lax.broadcasted_iota(jnp.int32, (ROWS, 32), 1) // RANK
    coefficient = jnp.where(member[...] == factor, proj, 0.0) * scale
    low_rank = jnp.dot(
        coefficient, right[...], precision=lax.Precision.HIGHEST, preferred_element_type=F32
    )
    out[...] = mine[...] + got[:, :IN_BLOCK].astype(F32) + low_rank


def output_block(mine, mine_proj, got, right_local, member_of):
    vmem = pl.BlockSpec(memory_space=pltpu.VMEM)
    return pl.pallas_call(
        functools.partial(output_kernel, perturb_scale / math.sqrt(RANK)),
        out_shape=jax.ShapeDtypeStruct((ROWS, IN_BLOCK), F32),
        in_specs=[vmem] * 5,
        out_specs=vmem,
        cost_estimate=pl.CostEstimate(
            flops=12 * ROWS * 32 * IN_BLOCK, bytes_accessed=2 * 2**20, transcendentals=0
        ),
    )(mine, mine_proj, got, right_local, member_of.reshape(ROWS, 1))


def on_device(tokens, base_weight, left_factors, right_factors, member_of, ranks):
    z, xl, core, y, xh = (lax.axis_index(name) for name in AXES)
    members = M_DEV * 64
    left = left_factors.reshape(32, IN_BLOCK)
    left_all = lax.all_gather(
        jnp.concatenate([left, rank_rows(ranks)]), "z", axis=0, tiled=True
    )

    offset = (y * 2 + xh) * IN_BLOCK
    right_local = lax.dynamic_slice_in_dim(right_factors, offset, IN_BLOCK, 2).reshape(32, IN_BLOCK)
    whole = spread_weights(base_weight, z, core)
    right = spread_right(right_local, z)
    held, swapped = ring(whole, core)
    blocks = spread_rows(jnp.concatenate([tokens, left.astype(BF16), right]), core)

    place = jnp.stack([z, core, xl ^ xh, y, xh]).astype(jnp.int32)
    mine, mine_proj, give = product(
        place, whole, *held[:3], *swapped[:3], held[3], swapped[3], *blocks
    )
    got = move(give, xl_target)
    outputs = output_block(mine, mine_proj, got, right_local, member_of)
    update = update_block(place, left_all, blocks, xl, members)
    return (outputs, update)


def solution(mesh):
    fine = Mesh(mesh.devices.reshape(tuple(SIZES.values())), AXES)
    return jax.shard_map(
        on_device,
        mesh=fine,
        in_specs=(
            P(POP, TENSOR),
            P(TENSOR, POP),
            P(POP, None, TENSOR),
            P(POP, None, None),
            P(POP, None),
            P(POP),
        ),
        out_specs=(P(POP, TENSOR), P(TENSOR, POP)),
        check_vma=False,
    )
```

```python
import functools
import itertools
import math

import jax
import jax.numpy as jnp
from jax import lax
from jax.experimental import pallas as pl
from jax.experimental.pallas import tpu as pltpu
from jax.sharding import Mesh
from jax.sharding import PartitionSpec as P

D = 5120
RANK = 4
M_DEV = 8
ROWS = 192
IN_BLOCK = 640
OUT_BLOCK = 80
EXTRA = 112
SLOT = 224

perturb_scale = 0.5

SIZES = {"z": 16, "xl": 2, "core": 2, "y": 4, "xh": 2}
AXES = tuple(SIZES)
POP = ("z", "xl", "core")
TENSOR = ("y", "xh")
BF16 = jnp.bfloat16
F32 = jnp.float32


def flat(place):
    index = 0
    for value, size in zip(place, SIZES.values()):
        index = index * size + value % size
    return index


def move(value, target):
    places = itertools.product(*(range(n) for n in SIZES.values()))
    return lax.ppermute(value, AXES, [(flat(p), flat(target(*p))) for p in places])


def weight_target(shift, z, xl, core, y, xh):
    owner = z // 2
    to_y, to_xh = owner // 2, owner % 2
    column = (z % 2) * 4 + xl * 2 + core
    near = (y - to_y) % 4
    return ((near // 2) * 8 + column + shift, xh, near % 2, to_y, to_xh)


def right_target(flip, z, xl, core, y, xh):
    half = z // 2
    return (2 * (2 * y + xh) + ((z % 2) ^ flip), half // 4, core, half % 4, xl)


def rows_target(flip, z, xl, core, y, xh):
    return (z, xh, core, y, xl ^ flip)


def z_target(step, z, xl, core, y, xh):
    return (z + step, xl, core, y, xh)


def core_target(z, xl, core, y, xh):
    return (z, xl, 1 - core, y, xh)


def xl_target(z, xl, core, y, xh):
    return (z, 1 - xl, core, y, xh)


def y_target(step, z, xl, core, y, xh):
    return (z, xl, core, y + step, xh)


def y_far_target(z, xl, core, y, xh):
    return (z, xl, core, y + (1 if core == 0 else -1), xh)


def nt_dot(a, b):
    return lax.dot_general(a, b, (((1,), (1,)), ((), ())), preferred_element_type=F32)


def split(value):
    high = lax.reduce_precision(value, 8, 7)
    return high.astype(BF16), (value - high).astype(BF16)


def slots_of(z):
    near = [(0, 0, 0), (0, SLOT, -1), (0, 2 * SLOT, 1)]
    far = [(1, 0, -2), (1, SLOT, 2), (1, 2 * SLOT, -3), (1, 3 * SLOT, 3)]
    return [(g, row, lax.rem(z + 16 + step, 8)) for g, row, step in near + far + [(2, 0, 4)]]


def product_kernel(
    place, g0, g1, g2, s0, s1, s2, t0, t1, t2, t3, mine, mine_proj, give, weights, total, proj
):
    z, core, own = place[0], place[1], place[2]
    for group, row, column in slots_of(z):
        rows = pl.ds(pl.multiple_of(column * OUT_BLOCK, 16), OUT_BLOCK)
        for half in range(2):
            start = row + half * (SLOT // 2)
            block = slice(start, start + OUT_BLOCK)
            weights[2 * half + core, rows, :] = (g0, g1, g2)[group][block, :]
            weights[2 * half + 1 - core, rows, :] = (s0, s1, s2)[group][block, :]

    for near, rows in enumerate((t0, t1, t2, t3)):
        part = nt_dot(rows[: 2 * ROWS, :], weights[near])
        total[...] = part if near == 0 else total[...] + part
        for m in range(2):
            left = rows[2 * ROWS + m * EXTRA : 2 * ROWS + m * EXTRA + 32, :]
            part = nt_dot(rows[m * ROWS : (m + 1) * ROWS, :], left)
            block = slice(m * ROWS, (m + 1) * ROWS)
            proj[block, :] = part if near == 0 else proj[block, :] + part
    here = pl.ds(pl.multiple_of(own * ROWS, ROWS), ROWS)
    there = pl.ds(pl.multiple_of((1 - own) * ROWS, ROWS), ROWS)
    mine[...] = total[here, :]
    mine_proj[...] = proj[here, :]
    give[:, :IN_BLOCK] = total[there, :].astype(BF16)
    give[:, IN_BLOCK:] = jnp.zeros((ROWS, 256), BF16)
    high = proj[there, :].astype(BF16)
    give[:, IN_BLOCK : IN_BLOCK + 32] = high
    give[:, IN_BLOCK + 128 : IN_BLOCK + 160] = (proj[there, :] - high.astype(F32)).astype(BF16)


def product(place, *arrays):
    vmem = pl.BlockSpec(memory_space=pltpu.VMEM)
    return pl.pallas_call(
        product_kernel,
        out_shape=(
            jax.ShapeDtypeStruct((ROWS, IN_BLOCK), F32),
            jax.ShapeDtypeStruct((ROWS, 32), F32),
            jax.ShapeDtypeStruct((ROWS, IN_BLOCK + 256), BF16),
        ),
        in_specs=[pl.BlockSpec(memory_space=pltpu.SMEM)] + [vmem] * len(arrays),
        out_specs=(vmem, vmem, vmem),
        scratch_shapes=[
            pltpu.VMEM((4, IN_BLOCK, IN_BLOCK), BF16),
            pltpu.VMEM((2 * ROWS, IN_BLOCK), F32),
            pltpu.VMEM((2 * ROWS, 32), F32),
        ],
        compiler_params=pltpu.CompilerParams(vmem_limit_bytes=40 * 2**20),
        cost_estimate=pl.CostEstimate(
            flops=2 * 384 * 640 * 2560, bytes_accessed=8 * 2**20, transcendentals=0
        ),
    )(place, *arrays)


def spread_columns(base_weight, left, z):
    piece = base_weight.T.astype(BF16)
    first = move(piece, functools.partial(weight_target, 0))
    second = move(piece, functools.partial(weight_target, 8))
    far = move(left, functools.partial(z_target, 8))
    slot = jnp.where(
        z < 8,
        jnp.concatenate([first, left, second, far]),
        jnp.concatenate([second, far, first, left]),
    )
    ups, downs = [slot], [slot]
    for _ in range(3):
        ups.append(move(ups[-1], functools.partial(z_target, 1)))
        downs.append(move(downs[-1], functools.partial(z_target, -1)))
    last_up = move(ups[3][: SLOT // 2], functools.partial(z_target, 1))
    last_down = move(downs[3][SLOT // 2 :], functools.partial(z_target, -1))
    groups = [
        jnp.concatenate([slot, ups[1], downs[1]]),
        jnp.concatenate([ups[2], downs[2], ups[3], downs[3]]),
        jnp.concatenate([last_up, last_down]),
    ]
    return groups, [move(g, core_target) for g in groups]


def spread_right(right_local, ranks, z):
    parity = z % 2
    levels = jnp.pad(ranks.astype(BF16)[None, :], ((0, 15), (0, 320 - M_DEV)))
    high, low = split(right_local)
    parts = []
    for flip in range(2):
        chunk = jnp.where(
            parity == flip,
            jnp.concatenate([high[:, :320], low[:, :320]]),
            jnp.concatenate([high[:, 320:], low[:, 320:]]),
        )
        sent = jnp.concatenate([chunk, levels])
        parts.append(move(sent, functools.partial(right_target, flip)))
    return jnp.concatenate(parts, 1)


def spread_rows(payload, core):
    a = move(payload, functools.partial(rows_target, 0))
    b = move(payload, functools.partial(rows_target, 1))
    near = jnp.concatenate([a[:ROWS], b[:ROWS], a[ROWS:], b[ROWS:]])
    above = move(near, functools.partial(y_target, -1))
    below = move(near, functools.partial(y_target, 1))
    far = move(jnp.where(core == 0, below, above), y_far_target)
    return near, above, far, below


def rank_kernel(*refs):
    out = refs[-1]
    lane = lax.broadcasted_iota(jnp.int32, (1, 128), 1)
    for i, ref in enumerate(refs[:-1]):
        row = ref[:, :384].astype(F32)[:1, :]
        out[i : i + 1, :128] = jnp.where(lane < M_DEV, row[:, :128], 0.0)
        second = jnp.logical_and(lane >= 64, lane < 64 + M_DEV)
        out[i : i + 1, 128:] = jnp.where(second, row[:, 256:384], 0.0)


def every_rank(blocks):
    rows = [(2 * ROWS + m * EXTRA + 96) // 16 for m in range(2)]
    specs = [pl.BlockSpec((16, IN_BLOCK), lambda i, r=r: (r, 0)) for r in rows]
    own = pl.pallas_call(
        rank_kernel,
        out_shape=jax.ShapeDtypeStruct((8, 256), F32),
        grid=(1,),
        in_specs=specs * 4,
        out_specs=pl.BlockSpec((8, 256), lambda i: (0, 0)),
        cost_estimate=pl.CostEstimate(flops=10000, bytes_accessed=200000, transcendentals=0),
    )(*[b for b in blocks for _ in range(2)])
    both = jnp.concatenate([own, move(own, core_target)])
    return both, move(both, xl_target)


def update_kernel(
    members, place, own, other, g0, g1, g2, t0, t1, t2, t3, keep, give, lefts, left, high, low, total
):
    z, core, y, xh = place[0], place[1], place[3], place[4]
    for group, row, column in slots_of(z):
        for half in range(2):
            start = row + half * (SLOT // 2) + OUT_BLOCK
            lefts[column + 8 * half] = (g0, g1, g2)[group][start : start + 32, :]

    rank_mean = (jnp.sum(own[...]) + jnp.sum(other[...])) / members
    lane = lax.broadcasted_iota(jnp.int32, (16, 256), 1)
    valid = jnp.logical_or(lane < M_DEV, jnp.logical_and(lane >= 192, lane < 192 + M_DEV))
    spread = jnp.where(valid, (own[...] - rank_mean) ** 2 + (other[...] - rank_mean) ** 2, 0.0)
    variance = jnp.full((8, 128), jnp.sum(spread) / members)
    scale = lax.rsqrt(variance + 1e-05)[:1, :1] * math.sqrt(D / (members * RANK))

    lane = lax.broadcasted_iota(jnp.int32, (32, 128), 1)
    member = lax.broadcasted_iota(jnp.int32, (32, 128), 0) // RANK
    in_first = lax.broadcasted_iota(jnp.int32, (32, IN_BLOCK), 1) < 320
    for near, extra in enumerate((t0, t1, t2, t3)):
        for m in range(2):
            index = near * 2 + m
            rows = slice(index * 32, index * 32 + 32)
            level = [
                jnp.sum(
                    jnp.where(
                        lane == member + 64 * flip,
                        own[index : index + 1, flip * 128 : flip * 128 + 128],
                        0.0,
                    ),
                    axis=1,
                    keepdims=True,
                )
                for flip in range(2)
            ]
            fitness = (jnp.where(in_first, level[0], level[1]) - rank_mean) * scale
            base = m * EXTRA
            scaled = fitness * (
                extra[base + 32 : base + 64, :].astype(F32)
                + extra[base + 64 : base + 96, :].astype(F32)
            )
            part = scaled.astype(BF16)
            high[rows, :] = part
            low[rows, :] = (scaled - part.astype(F32)).astype(BF16)
            pair = (xh ^ m) * 4 + lax.rem(y + near, 4)
            for flip in range(2):
                left[flip, rows, :] = lefts[2 * pair + (lax.rem(z, 2) ^ flip)]

    def tn_dot(a, b):
        return lax.dot_general(a, b, (((0,), (0,)), ((), ())), preferred_element_type=F32)

    total[...] = (tn_dot(high[:, :384], left[0]) + tn_dot(low[:, :384], left[0]))[:320]
    total[...] += (tn_dot(high[:, 256:], left[1]) + tn_dot(low[:, 256:], left[1]))[64:]
    for i in range(2):
        here = pl.ds(pl.multiple_of((2 * i + core) * OUT_BLOCK, 8), OUT_BLOCK)
        there = pl.ds(pl.multiple_of((2 * i + 1 - core) * OUT_BLOCK, 8), OUT_BLOCK)
        keep[i] = total[here, :]
        give[i] = total[there, :]


def update_block(place, groups, blocks, xl, members):
    vmem = pl.BlockSpec(memory_space=pltpu.VMEM)
    shape = jax.ShapeDtypeStruct((2, OUT_BLOCK, IN_BLOCK), F32)
    extras = [b[2 * ROWS :] for b in blocks]
    keep, give = pl.pallas_call(
        functools.partial(update_kernel, members),
        out_shape=(shape, shape),
        in_specs=[pl.BlockSpec(memory_space=pltpu.SMEM)] + [vmem] * 9,
        out_specs=(vmem, vmem),
        scratch_shapes=[
            pltpu.VMEM((16, 32, IN_BLOCK), BF16),
            pltpu.VMEM((2, 256, IN_BLOCK), BF16),
            pltpu.VMEM((256, IN_BLOCK), BF16),
            pltpu.VMEM((256, IN_BLOCK), BF16),
            pltpu.VMEM((320, IN_BLOCK), F32),
        ],
        compiler_params=pltpu.CompilerParams(vmem_limit_bytes=32 * 2**20),
        cost_estimate=pl.CostEstimate(
            flops=8 * 384 * 256 * 640, bytes_accessed=4 * 2**20, transcendentals=0
        ),
    )(place, *every_rank(blocks), *groups, *extras)
    keep = keep + move(give, core_target)
    give = jnp.where(xl == 0, keep[1], keep[0])
    keep = jnp.where(xl == 0, keep[0], keep[1])
    return (keep + move(give, xl_target)).T


def output_kernel(scale, mine, mine_proj, got, right, member, out):
    proj = mine_proj[...]
    proj += got[:, IN_BLOCK : IN_BLOCK + 32].astype(F32)
    proj += got[:, IN_BLOCK + 128 : IN_BLOCK + 160].astype(F32)
    factor = lax.broadcasted_iota(jnp.int32, (ROWS, 32), 1) // RANK
    coefficient = jnp.where(member[...] == factor, proj, 0.0) * scale
    low_rank = jnp.dot(
        coefficient, right[...], precision=lax.Precision.HIGHEST, preferred_element_type=F32
    )
    out[...] = mine[...] + got[:, :IN_BLOCK].astype(F32) + low_rank


def output_block(mine, mine_proj, got, right_local, member_of):
    vmem = pl.BlockSpec(memory_space=pltpu.VMEM)
    return pl.pallas_call(
        functools.partial(output_kernel, perturb_scale / math.sqrt(RANK)),
        out_shape=jax.ShapeDtypeStruct((ROWS, IN_BLOCK), F32),
        in_specs=[vmem] * 5,
        out_specs=vmem,
        cost_estimate=pl.CostEstimate(
            flops=12 * ROWS * 32 * IN_BLOCK, bytes_accessed=2 * 2**20, transcendentals=0
        ),
    )(mine, mine_proj, got, right_local, member_of.reshape(ROWS, 1))


def on_device(tokens, base_weight, left_factors, right_factors, member_of, ranks):
    z, xl, core, y, xh = (lax.axis_index(name) for name in AXES)
    members = M_DEV * 64
    left = left_factors.astype(BF16).reshape(32, IN_BLOCK)
    offset = (y * 2 + xh) * IN_BLOCK
    right_local = lax.dynamic_slice_in_dim(right_factors, offset, IN_BLOCK, 2).reshape(32, IN_BLOCK)
    right = spread_right(right_local, ranks, z)
    groups, swapped = spread_columns(base_weight, left, z)
    blocks = spread_rows(jnp.concatenate([tokens, left, right]), core)

    place = jnp.stack([z, core, xl ^ xh, y, xh]).astype(jnp.int32)
    mine, mine_proj, give = product(place, *groups, *swapped, *blocks)
    got = move(give, xl_target)
    outputs = output_block(mine, mine_proj, got, right_local, member_of)
    update = update_block(place, groups, blocks, xl, members)
    return (outputs, update)


def solution(mesh):
    fine = Mesh(mesh.devices.reshape(tuple(SIZES.values())), AXES)
    return jax.shard_map(
        on_device,
        mesh=fine,
        in_specs=(
            P(POP, TENSOR),
            P(TENSOR, POP),
            P(POP, None, TENSOR),
            P(POP, None, None),
            P(POP, None),
            P(POP),
        ),
        out_specs=(P(POP, TENSOR), P(TENSOR, POP)),
        check_vma=False,
    )
```

```python
import functools
import itertools
import math

import jax
import jax.numpy as jnp
from jax import lax
from jax.experimental import pallas as pl
from jax.experimental.pallas import tpu as pltpu
from jax.sharding import Mesh
from jax.sharding import PartitionSpec as P

D = 5120
RANK = 4
M_DEV = 8
ROWS = 192
IN_BLOCK = 640
OUT_BLOCK = 80
SLOT = 224
EXTRA = 80
LEFT_AT = 2 * EXTRA
ROWS_AT = LEFT_AT + 64
SEND = IN_BLOCK + 128

perturb_scale = 0.5

SIZES = {"z": 16, "xl": 2, "core": 2, "y": 4, "xh": 2}
AXES = tuple(SIZES)
POP = ("z", "xl", "core")
TENSOR = ("y", "xh")
BF16 = jnp.bfloat16
F32 = jnp.float32


def flat(place):
    index = 0
    for value, size in zip(place, SIZES.values()):
        index = index * size + value % size
    return index


def move(value, target):
    places = itertools.product(*(range(n) for n in SIZES.values()))
    return lax.ppermute(value, AXES, [(flat(p), flat(target(*p))) for p in places])


def weight_target(z, xl, core, y, xh):
    owner = z // 2
    to_y, to_xh = owner // 2, owner % 2
    column = (z % 2) * 4 + xl * 2 + core
    near = (y - to_y) % 4
    return ((near // 2) * 8 + column, xh, near % 2, to_y, to_xh)


def right_target(z, xl, core, y, xh):
    return (2 * (2 * y + xh) + z % 2, xl, core, z // 4, z // 2 % 2)


def rows_target(flip, z, xl, core, y, xh):
    return (z, xh, core, y, xl ^ flip)


def z_target(step, z, xl, core, y, xh):
    return (z + step, xl, core, y, xh)


def core_target(z, xl, core, y, xh):
    return (z, xl, 1 - core, y, xh)


def z_pair_target(z, xl, core, y, xh):
    return (z ^ 1, xl, core, y, xh)


def xh_target(z, xl, core, y, xh):
    return (z, xl, core, y, 1 - xh)


def xl_target(z, xl, core, y, xh):
    return (z, 1 - xl, core, y, xh)


def y_target(step, z, xl, core, y, xh):
    return (z, xl, core, y + step, xh)


def y_far_target(z, xl, core, y, xh):
    return (z, xl, core, y + (1 if core == 0 else -1), xh)


def nt_dot(a, b):
    return lax.dot_general(a, b, (((1,), (1,)), ((), ())), preferred_element_type=F32)


def split(value):
    high = lax.reduce_precision(value, 8, 7)
    return high.astype(BF16), (value - high).astype(BF16)


SLOT_STEPS = (0, -1, 1, -2, 2, -3, 3)


def slot_halves(z, refs):
    for ref, step in zip(refs, SLOT_STEPS):
        for half in range(2):
            yield lax.rem(z + 16 + step, 8), half, ref, half * (SLOT // 2)
    for half in range(2):
        yield lax.rem(z + 4, 8), half, refs[len(SLOT_STEPS) + half], 0


def paired(proj):
    lane = lax.broadcasted_iota(jnp.int32, proj.shape, 1)
    first = jnp.where(lane < 32, proj, 0.0)
    high = first.astype(BF16).astype(F32)
    return (high + pltpu.roll(first - high, 32, 1)).astype(BF16)


def unpaired(value):
    value = value.astype(F32)
    return value + pltpu.roll(value, 96, 1)


def product_kernel(place, *refs):
    slots, (t0, t1, t2, t3, p0, p1) = refs[:9], refs[9:15]
    mine, mine_proj, give, weights, rows = refs[15:]
    z, core = place[0], place[1]
    for column, half, ref, start in slot_halves(z, slots):
        at = pl.ds(pl.multiple_of(column * OUT_BLOCK, 16), OUT_BLOCK)
        weights[half, at, :] = ref[start : start + OUT_BLOCK, :]

    @pl.when(core == 0)
    def _():
        rows[0] = t0[LEFT_AT:, :]
        rows[1] = t2[LEFT_AT:, :]

    @pl.when(core == 1)
    def _():
        rows[0] = t1[LEFT_AT:, :]
        rows[1] = t3[LEFT_AT:, :]

    def sums(a, b):
        total = nt_dot(a[64:], weights[0]) + nt_dot(b[64:], weights[1])
        proj = []
        for m in range(2):
            part = 0.0
            for block in (a, b):
                left = block[m * 32 : m * 32 + 32]
                left = jnp.concatenate([left] * 4)
                part = part + nt_dot(block[64 + m * ROWS : 64 + (m + 1) * ROWS], left)
            proj.append(part)
        return total, jnp.concatenate(proj)

    total, proj = sums(p0[...], p1[...])
    give[:, :IN_BLOCK] = total.astype(BF16)
    give[:, IN_BLOCK:] = paired(proj)
    total, proj = sums(rows[0], rows[1])
    mine[...] = total
    mine_proj[...] = proj


def product(place, *arrays):
    vmem = pl.BlockSpec(memory_space=pltpu.VMEM)
    return pl.pallas_call(
        product_kernel,
        out_shape=(
            jax.ShapeDtypeStruct((2 * ROWS, IN_BLOCK), F32),
            jax.ShapeDtypeStruct((2 * ROWS, 128), F32),
            jax.ShapeDtypeStruct((2 * ROWS, SEND), BF16),
        ),
        in_specs=[pl.BlockSpec(memory_space=pltpu.SMEM)] + [vmem] * len(arrays),
        out_specs=(vmem, vmem, vmem),
        scratch_shapes=[
            pltpu.VMEM((2, IN_BLOCK, IN_BLOCK), BF16),
            pltpu.VMEM((2, 64 + 2 * ROWS, IN_BLOCK), BF16),
        ],
        compiler_params=pltpu.CompilerParams(vmem_limit_bytes=40 * 2**20),
        cost_estimate=pl.CostEstimate(
            flops=2 * 768 * 640 * 1280, bytes_accessed=8 * 2**20, transcendentals=0
        ),
    )(place, *arrays)


def join_kernel(place, total, proj, got, mine, mine_proj, give):
    own = place[2]
    for block, to_give in ((own, False), (1 - own, True)):
        at = pl.ds(pl.multiple_of(block * ROWS, ROWS), ROWS)
        value = total[at, :] + got[at, :IN_BLOCK].astype(F32)
        sums = proj[at, :] + unpaired(got[at, IN_BLOCK:])
        if to_give:
            give[:, :IN_BLOCK] = value.astype(BF16)
            give[:, IN_BLOCK:] = paired(sums)
        else:
            mine[...] = value
            mine_proj[...] = sums


def join(place, total, proj, got):
    vmem = pl.BlockSpec(memory_space=pltpu.VMEM)
    return pl.pallas_call(
        join_kernel,
        out_shape=(
            jax.ShapeDtypeStruct((ROWS, IN_BLOCK), F32),
            jax.ShapeDtypeStruct((ROWS, 128), F32),
            jax.ShapeDtypeStruct((ROWS, SEND), BF16),
        ),
        in_specs=[pl.BlockSpec(memory_space=pltpu.SMEM)] + [vmem] * 3,
        out_specs=(vmem, vmem, vmem),
        cost_estimate=pl.CostEstimate(flops=10**6, bytes_accessed=3 * 2**20, transcendentals=0),
    )(place, total, proj, got)


def spread_columns(base_weight, left, z):
    piece = move(base_weight.T.astype(BF16), weight_target)
    half = jnp.concatenate([piece, left])
    far = move(half, functools.partial(z_target, 8))
    slot = jnp.where(z < 8, jnp.concatenate([half, far]), jnp.concatenate([far, half]))
    up = down = slot
    slots = [slot]
    for _ in range(3):
        up = move(up, functools.partial(z_target, 1))
        down = move(down, functools.partial(z_target, -1))
        slots += [up, down]
    last_up = move(up[: SLOT // 2], functools.partial(z_target, 1))
    last_down = move(down[SLOT // 2 :], functools.partial(z_target, -1))
    return slots + [last_up, last_down]


def rank_row(ranks):
    own = jnp.pad(ranks.astype(BF16)[None, :], ((0, 15), (0, 120)))
    both = jnp.concatenate([own[:, :M_DEV], move(own, core_target)[:, :M_DEV]], 1)
    both = jnp.pad(both, ((0, 0), (0, 112)))
    every = jnp.concatenate([both[:, : 2 * M_DEV], move(both, xl_target)[:, : 2 * M_DEV]], 1)
    return jnp.pad(every, ((0, 0), (0, IN_BLOCK - 4 * M_DEV)))


def spread_right(right_local, ranks, z):
    sent = jnp.concatenate([*split(right_local), rank_row(ranks)])
    got = move(sent, right_target)
    odd = z % 2 == 1
    levels = got[64:, :320]
    own = jnp.where(odd, got[:64, 320:], got[:64, :320])
    other = jnp.where(odd, got[:64, :320], got[:64, 320:])
    pair = move(jnp.concatenate([other, levels]), z_pair_target)
    both = jnp.concatenate([jnp.concatenate([own, levels]), pair], 1)
    return jnp.concatenate([both, move(both, xh_target)])


def spread_rows(tokens, left, right, core):
    payload = jnp.concatenate([left, tokens])
    a = move(payload, functools.partial(rows_target, 0))
    b = move(payload, functools.partial(rows_target, 1))
    near = jnp.concatenate([right, a[:32], b[:32], a[32:], b[32:]])
    above = move(near, functools.partial(y_target, -1))
    below = move(near, functools.partial(y_target, 1))
    far = move(jnp.where(core == 0, below, above), y_far_target)
    first = move(jnp.where(core == 0, above[LEFT_AT:], near[LEFT_AT:]), core_target)
    second = move(jnp.where(core == 0, below[LEFT_AT:], far[LEFT_AT:]), core_target)
    return (near, above, far, below), (first, second)


def update_kernel(members, place, *refs):
    slots, extras = refs[:9], refs[9:13]
    keep, give, lefts, left, high, low, total = refs[13:]
    z, core, y, xh = place[0], place[1], place[3], place[4]
    for column, half, ref, start in slot_halves(z, slots):
        lefts[column + 8 * half] = ref[start + OUT_BLOCK : start + SLOT // 2, :]

    lane = lax.broadcasted_iota(jnp.int32, (1, 128), 1)
    levels, spread, rank_sum = [], 0.0, 0.0
    for extra in extras:
        for h in range(2):
            row = extra[h * EXTRA + 64 : h * EXTRA + EXTRA, :384].astype(F32)[:1, :]
            pair = [
                (row[:, 256 * f : 256 * f + 128], jnp.logical_and(lane >= 64 * f, lane < 64 * f + 32))
                for f in range(2)
            ]
            levels.append(pair)
    for value, valid in sum(levels, []):
        rank_sum = rank_sum + jnp.where(valid, value, 0.0)
    rank_mean = jnp.sum(rank_sum) / members
    for value, valid in sum(levels, []):
        spread = spread + jnp.where(valid, (value - rank_mean) ** 2, 0.0)
    variance = jnp.full((8, 128), jnp.sum(spread) / members)
    scale = lax.rsqrt(variance + 1e-05)[:1, :1] * math.sqrt(D / (members * RANK))

    lane = lax.broadcasted_iota(jnp.int32, (32, 128), 1)
    member = lax.broadcasted_iota(jnp.int32, (32, 128), 0) // RANK
    in_first = lax.broadcasted_iota(jnp.int32, (32, IN_BLOCK), 1) < 320
    for near, extra in enumerate(extras):
        for h in range(2):
            index = near * 2 + h
            rows = slice(index * 32, index * 32 + 32)
            level = [
                jnp.sum(jnp.where(lane == member + 64 * f, value, 0.0), axis=1, keepdims=True)
                for f, (value, _) in enumerate(levels[index])
            ]
            fitness = (jnp.where(in_first, level[0], level[1]) - rank_mean) * scale
            base = h * EXTRA
            scaled = fitness * (
                extra[base : base + 32, :].astype(F32) + extra[base + 32 : base + 64, :].astype(F32)
            )
            part = scaled.astype(BF16)
            high[rows, :] = part
            low[rows, :] = (scaled - part.astype(F32)).astype(BF16)
            pair = 2 * lax.rem(y + near, 4) + (xh ^ h)
            for flip in range(2):
                left[flip, rows, :] = lefts[2 * pair + (lax.rem(z, 2) ^ flip)]

    def tn_dot(a, b):
        return lax.dot_general(a, b, (((0,), (0,)), ((), ())), preferred_element_type=F32)

    total[...] = (tn_dot(high[:, :384], left[0]) + tn_dot(low[:, :384], left[0]))[:320]
    total[...] += (tn_dot(high[:, 256:], left[1]) + tn_dot(low[:, 256:], left[1]))[64:]
    for i in range(2):
        here = pl.ds(pl.multiple_of((2 * i + core) * OUT_BLOCK, 8), OUT_BLOCK)
        there = pl.ds(pl.multiple_of((2 * i + 1 - core) * OUT_BLOCK, 8), OUT_BLOCK)
        keep[i] = total[here, :]
        give[i] = total[there, :]


def update_block(place, slots, blocks, xl, members):
    vmem = pl.BlockSpec(memory_space=pltpu.VMEM)
    extra = pl.BlockSpec((LEFT_AT, IN_BLOCK), lambda i: (0, 0))
    shape = jax.ShapeDtypeStruct((2, OUT_BLOCK, IN_BLOCK), F32)
    keep, give = pl.pallas_call(
        functools.partial(update_kernel, members),
        out_shape=(shape, shape),
        grid=(1,),
        in_specs=[pl.BlockSpec(memory_space=pltpu.SMEM)] + [vmem] * 9 + [extra] * 4,
        out_specs=(vmem, vmem),
        scratch_shapes=[
            pltpu.VMEM((16, 32, IN_BLOCK), BF16),
            pltpu.VMEM((2, 256, IN_BLOCK), BF16),
            pltpu.VMEM((256, IN_BLOCK), BF16),
            pltpu.VMEM((256, IN_BLOCK), BF16),
            pltpu.VMEM((320, IN_BLOCK), F32),
        ],
        compiler_params=pltpu.CompilerParams(vmem_limit_bytes=32 * 2**20),
        cost_estimate=pl.CostEstimate(
            flops=8 * 384 * 256 * 640, bytes_accessed=4 * 2**20, transcendentals=0
        ),
    )(place, *slots, *blocks)
    keep = keep + move(give, core_target)
    give = jnp.where(xl == 0, keep[1], keep[0])
    keep = jnp.where(xl == 0, keep[0], keep[1])
    return (keep + move(give, xl_target)).T


def output_kernel(scale, mine, mine_proj, got, right, member, out):
    proj = mine_proj[...] + unpaired(got[:, IN_BLOCK:])
    factor = lax.broadcasted_iota(jnp.int32, (ROWS, 128), 1) // RANK
    coefficient = jnp.where(member[...] == factor, proj, 0.0)[:, :32] * scale
    low_rank = jnp.dot(
        coefficient, right[...], precision=lax.Precision.HIGHEST, preferred_element_type=F32
    )
    out[...] = mine[...] + got[:, :IN_BLOCK].astype(F32) + low_rank


def output_block(mine, mine_proj, got, right_local, member_of):
    vmem = pl.BlockSpec(memory_space=pltpu.VMEM)
    return pl.pallas_call(
        functools.partial(output_kernel, perturb_scale / math.sqrt(RANK)),
        out_shape=jax.ShapeDtypeStruct((ROWS, IN_BLOCK), F32),
        in_specs=[vmem] * 5,
        out_specs=vmem,
        cost_estimate=pl.CostEstimate(
            flops=12 * ROWS * 32 * IN_BLOCK, bytes_accessed=2 * 2**20, transcendentals=0
        ),
    )(mine, mine_proj, got, right_local, member_of.reshape(ROWS, 1))


def on_device(tokens, base_weight, left_factors, right_factors, member_of, ranks):
    z, xl, core, y, xh = (lax.axis_index(name) for name in AXES)
    members = M_DEV * 64
    left = left_factors.astype(BF16).reshape(32, IN_BLOCK)
    offset = (y * 2 + xh) * IN_BLOCK
    right_local = lax.dynamic_slice_in_dim(right_factors, offset, IN_BLOCK, 2).reshape(32, IN_BLOCK)
    slots = spread_columns(base_weight, left, z)
    right = spread_right(right_local, ranks, z)
    blocks, others = spread_rows(tokens, left, right, core)

    place = jnp.stack([z, core, xl ^ xh, y, xh]).astype(jnp.int32)
    total, proj, give = product(place, *slots, *blocks, *others)
    mine, mine_proj, give = join(place, total, proj, move(give, core_target))
    got = move(give, xl_target)
    outputs = output_block(mine, mine_proj, got, right_local, member_of)
    update = update_block(place, slots, blocks, xl, members)
    return (outputs, update)


def solution(mesh):
    fine = Mesh(mesh.devices.reshape(tuple(SIZES.values())), AXES)
    return jax.shard_map(
        on_device,
        mesh=fine,
        in_specs=(
            P(POP, TENSOR),
            P(TENSOR, POP),
            P(POP, None, TENSOR),
            P(POP, None, None),
            P(POP, None),
            P(POP),
        ),
        out_specs=(P(POP, TENSOR), P(TENSOR, POP)),
        check_vma=False,
    )
```

```python
import functools
import itertools
import math

import jax
import jax.numpy as jnp
from jax import lax
from jax.experimental import pallas as pl
from jax.experimental.pallas import tpu as pltpu
from jax.sharding import Mesh
from jax.sharding import PartitionSpec as P

D = 5120
RANK = 4
M_DEV = 8
ROWS = 192
IN_BLOCK = 640
OUT_BLOCK = 80
SLOT = 112
EXTRA = 80
SEND = IN_BLOCK + 128

perturb_scale = 0.5

SIZES = {"z": 16, "xl": 2, "core": 2, "y": 4, "xh": 2}
AXES = tuple(SIZES)
POP = ("z", "xl", "core")
TENSOR = ("y", "xh")
BF16 = jnp.bfloat16
F32 = jnp.float32


def flat(place):
    index = 0
    for value, size in zip(place, SIZES.values()):
        index = index * size + value % size
    return index


def move(value, target):
    places = itertools.product(*(range(n) for n in SIZES.values()))
    return lax.ppermute(value, AXES, [(flat(p), flat(target(*p))) for p in places])


def weight_target(z, xl, core, y, xh):
    owner = z // 2
    to_y, to_xh = owner // 2, owner % 2
    column = (z % 2) * 4 + xl * 2 + core
    near = (y - to_y) % 4
    return ((near % 2) * 8 + column, xh, near // 2, to_y, to_xh)


def right_target(z, xl, core, y, xh):
    return (2 * (2 * y + xh) + z % 2, xl, core, z // 4, z // 2 % 2)


def rows_target(flip, z, xl, core, y, xh):
    return (z, xh, core, y, xl ^ flip)


def z_target(step, z, xl, core, y, xh):
    return (z + step, xl, core, y, xh)


def core_target(z, xl, core, y, xh):
    return (z, xl, 1 - core, y, xh)


def z_pair_target(z, xl, core, y, xh):
    return (z ^ 1, xl, core, y, xh)


def xh_target(z, xl, core, y, xh):
    return (z, xl, core, y, 1 - xh)


def xl_target(z, xl, core, y, xh):
    return (z, 1 - xl, core, y, xh)


def y_pair_target(z, xl, core, y, xh):
    return (z, xl, core, y ^ 1, xh)


def y_half_target(z, xl, core, y, xh):
    return (z, xl, core, y + 2, xh)


def y_apart_target(z, xl, core, y, xh):
    return (z, xl, core, y + (1 if core else -1), xh)


def y_forward_target(z, xl, core, y, xh):
    return (z, xl, core, y + core, xh)


def nt_dot(a, b):
    return lax.dot_general(a, b, (((1,), (1,)), ((), ())), preferred_element_type=F32)


def split(value):
    high = lax.reduce_precision(value, 8, 7)
    return high.astype(BF16), (value - high).astype(BF16)


def paired(proj):
    lane = lax.broadcasted_iota(jnp.int32, proj.shape, 1)
    first = jnp.where(lane < 32, proj, 0.0)
    high = first.astype(BF16).astype(F32)
    return (high + pltpu.roll(first - high, 32, 1)).astype(BF16)


def unpaired(value):
    value = value.astype(F32)
    return value + pltpu.roll(value, 96, 1)


def main_kernel(members, place, *refs):
    slots, near, step, forward, right = refs[:5]
    mine, mine_proj, keep, give = refs[5:9]
    weights, rows, left, high, low, total = refs[9:]
    core = place[1]
    for half in range(2):
        for column in range(8):
            start = (half * 8 + column) * SLOT
            at = slice(column * OUT_BLOCK, (column + 1) * OUT_BLOCK)
            weights[half, at, :] = slots[start : start + OUT_BLOCK, :]

    @pl.when(core == 0)
    def _():
        rows[...] = near[...]

    @pl.when(core == 1)
    def _():
        rows[...] = forward[...]

    def sums(base):
        x = slice(base + 64, base + 64 + 2 * ROWS)
        block = nt_dot(rows[x, :], weights[0]) + nt_dot(step[x, :], weights[1])
        proj = []
        for m in range(2):
            part = 0.0
            for ref in (rows, step):
                factor = ref[base + m * 32 : base + m * 32 + 32, :]
                x = slice(base + 64 + m * ROWS, base + 64 + (m + 1) * ROWS)
                part = part + nt_dot(ref[x, :], jnp.concatenate([factor] * 4))
            proj.append(part)
        return block, jnp.concatenate(proj)

    block, proj = sums(2 * ROWS + 64)
    give[: 2 * ROWS, :IN_BLOCK] = block.astype(BF16)
    give[: 2 * ROWS, IN_BLOCK:] = paired(proj)
    block, proj = sums(0)
    mine[...] = block
    mine_proj[...] = proj

    update_sums(members, place, slots, right, left, high, low, total)
    for i in range(2):
        here = pl.ds(pl.multiple_of((2 * i + core) * OUT_BLOCK, 8), OUT_BLOCK)
        there = pl.ds(pl.multiple_of((2 * i + 1 - core) * OUT_BLOCK, 8), OUT_BLOCK)
        keep[i * OUT_BLOCK : (i + 1) * OUT_BLOCK, :] = total[here, :]
        put_pair(give, 2 * ROWS + 2 * i * OUT_BLOCK, total[there, :])


def put_pair(ref, start, value):
    part = value.astype(BF16)
    ref[start : start + OUT_BLOCK, :IN_BLOCK] = part
    ref[start + OUT_BLOCK : start + 2 * OUT_BLOCK, :IN_BLOCK] = (value - part.astype(F32)).astype(BF16)
    ref[start : start + 2 * OUT_BLOCK, IN_BLOCK:] = jnp.zeros((2 * OUT_BLOCK, SEND - IN_BLOCK), BF16)


def take_pair(ref, start):
    block = ref[start : start + 2 * OUT_BLOCK, :IN_BLOCK].astype(F32)
    return block[:OUT_BLOCK] + block[OUT_BLOCK:]


def main(place, members, *arrays):
    vmem = pl.BlockSpec(memory_space=pltpu.VMEM)
    return pl.pallas_call(
        functools.partial(main_kernel, members),
        out_shape=(
            jax.ShapeDtypeStruct((2 * ROWS, IN_BLOCK), F32),
            jax.ShapeDtypeStruct((2 * ROWS, 128), F32),
            jax.ShapeDtypeStruct((2 * OUT_BLOCK, IN_BLOCK), F32),
            jax.ShapeDtypeStruct((2 * ROWS + 4 * OUT_BLOCK, SEND), BF16),
        ),
        in_specs=[pl.BlockSpec(memory_space=pltpu.SMEM)] + [vmem] * len(arrays),
        out_specs=(vmem,) * 4,
        scratch_shapes=[
            pltpu.VMEM((2, IN_BLOCK, IN_BLOCK), BF16),
            pltpu.VMEM((2 * (64 + 2 * ROWS), IN_BLOCK), BF16),
            pltpu.VMEM((2, 256, IN_BLOCK), BF16),
            pltpu.VMEM((256, IN_BLOCK), BF16),
            pltpu.VMEM((256, IN_BLOCK), BF16),
            pltpu.VMEM((320, IN_BLOCK), F32),
        ],
        compiler_params=pltpu.CompilerParams(vmem_limit_bytes=56 * 2**20),
        cost_estimate=pl.CostEstimate(
            flops=2 * 768 * 640 * 1280, bytes_accessed=10 * 2**20, transcendentals=0
        ),
    )(place, *arrays)


def join_kernel(place, total, proj, keep, got, mine, mine_proj, mine_update, give):
    own, xl = place[2], place[5]
    for block, to_give in ((own, False), (1 - own, True)):
        at = pl.ds(pl.multiple_of(block * ROWS, ROWS), ROWS)
        value = total[at, :] + got[at, :IN_BLOCK].astype(F32)
        sums = proj[at, :] + unpaired(got[at, IN_BLOCK:])
        if to_give:
            give[:ROWS, :IN_BLOCK] = value.astype(BF16)
            give[:ROWS, IN_BLOCK:] = paired(sums)
        else:
            mine[...] = value
            mine_proj[...] = sums
    update = [
        keep[i * OUT_BLOCK : (i + 1) * OUT_BLOCK, :] + take_pair(got, 2 * ROWS + 2 * i * OUT_BLOCK)
        for i in range(2)
    ]
    mine_update[...] = jnp.where(xl == 0, update[0], update[1])
    put_pair(give, ROWS, jnp.where(xl == 0, update[1], update[0]))


def join(place, total, proj, keep, got):
    vmem = pl.BlockSpec(memory_space=pltpu.VMEM)
    return pl.pallas_call(
        join_kernel,
        out_shape=(
            jax.ShapeDtypeStruct((ROWS, IN_BLOCK), F32),
            jax.ShapeDtypeStruct((ROWS, 128), F32),
            jax.ShapeDtypeStruct((OUT_BLOCK, IN_BLOCK), F32),
            jax.ShapeDtypeStruct((ROWS + 2 * OUT_BLOCK, SEND), BF16),
        ),
        in_specs=[pl.BlockSpec(memory_space=pltpu.SMEM)] + [vmem] * 4,
        out_specs=(vmem,) * 4,
        compiler_params=pltpu.CompilerParams(vmem_limit_bytes=56 * 2**20),
        cost_estimate=pl.CostEstimate(flops=10**6, bytes_accessed=4 * 2**20, transcendentals=0),
    )(place, total, proj, keep, got)


def after(value, other):
    there = other[0, 0] == other[0, 0]
    return jnp.where(there, value, jnp.zeros_like(value))


def rank_row(ranks):
    own = jnp.pad(ranks.astype(BF16)[None, :], ((0, 15), (0, 120)))
    every = lax.all_gather(own, ("xl", "core"), axis=1, tiled=True)
    every = jnp.concatenate([every[:, g * 128 : g * 128 + M_DEV] for g in range(4)], 1)
    return jnp.pad(every, ((0, 0), (0, IN_BLOCK - 4 * M_DEV)))


def spread_right(right_local, ranks, slot, z):
    sent = jnp.concatenate([*split(right_local), rank_row(ranks)])
    got = move(sent, right_target)
    odd = z % 2 == 1
    levels = got[64:, :320]
    own = jnp.where(odd, got[:64, 320:], got[:64, :320])
    other = jnp.where(odd, got[:64, :320], got[:64, 320:])
    pair = move(after(jnp.concatenate([other, levels]), slot), z_pair_target)
    held = jnp.concatenate([jnp.concatenate([own, levels]), pair], 1)
    for target in (xh_target, y_pair_target, y_half_target):
        held = jnp.concatenate([held, move(held, target)])
    return held


def spread_rows(tokens, left, slot):
    payload = after(jnp.concatenate([left, tokens]), slot)
    a = move(payload, functools.partial(rows_target, 0))
    b = move(payload, functools.partial(rows_target, 1))
    near = jnp.concatenate([a[:32], b[:32], a[32:], b[32:]])
    near = jnp.concatenate([near, move(near, core_target)])
    step = move(near, y_apart_target)
    return near, step, move(step, y_forward_target)


def update_sums(members, place, slots, right, left, high, low, total):
    z, core, y, xh, xl = place[0], place[1], place[3], place[4], place[5]
    blocks = [(far, pair, h) for far in range(2) for pair in range(2) for h in range(2)]
    lane = lax.broadcasted_iota(jnp.int32, (1, 128), 1)
    levels, spread, rank_sum = [], 0.0, 0.0
    for index in range(8):
        row = right[index * EXTRA + 64 : index * EXTRA + EXTRA, :384].astype(F32)[:1, :]
        pair = [
            (row[:, 256 * f : 256 * f + 128], jnp.logical_and(lane >= 64 * f, lane < 64 * f + 32))
            for f in range(2)
        ]
        levels.append(pair)
    for value, valid in sum(levels, []):
        rank_sum = rank_sum + jnp.where(valid, value, 0.0)
    rank_mean = jnp.sum(rank_sum) / members
    for value, valid in sum(levels, []):
        spread = spread + jnp.where(valid, (value - rank_mean) ** 2, 0.0)
    variance = jnp.full((8, 128), jnp.sum(spread) / members)
    scale = lax.rsqrt(variance + 1e-05)[:1, :1] * math.sqrt(D / (members * RANK))

    lane = lax.broadcasted_iota(jnp.int32, (32, 128), 1)
    member = lax.broadcasted_iota(jnp.int32, (32, 128), 0) // RANK
    in_first = lax.broadcasted_iota(jnp.int32, (32, IN_BLOCK), 1) < 320
    for index, (far, pair, h) in enumerate(blocks):
        rows = slice(index * 32, index * 32 + 32)
        own = member + 8 * (2 * xl + core)
        level = [
            jnp.sum(jnp.where(lane == own + 64 * f, value, 0.0), axis=1, keepdims=True)
            for f, (value, _) in enumerate(levels[index])
        ]
        fitness = (jnp.where(in_first, level[0], level[1]) - rank_mean) * scale
        base = index * EXTRA
        scaled = fitness * (
            right[base : base + 32, :].astype(F32) + right[base + 32 : base + 64, :].astype(F32)
        )
        part = scaled.astype(BF16)
        high[rows, :] = part
        low[rows, :] = (scaled - part.astype(F32)).astype(BF16)
        source = 2 * lax.rem((y ^ pair) + 2 * far, 4) + (xh ^ h)
        for flip in range(2):
            start = (2 * source + (lax.rem(z, 2) ^ flip)) * SLOT + OUT_BLOCK
            left[flip, rows, :] = slots[pl.ds(pl.multiple_of(start, 16), 32), :]

    def tn_dot(a, b):
        return lax.dot_general(a, b, (((0,), (0,)), ((), ())), preferred_element_type=F32)

    total[...] = (tn_dot(high[:, :384], left[0]) + tn_dot(low[:, :384], left[0]))[:320]
    total[...] += (tn_dot(high[:, 256:], left[1]) + tn_dot(low[:, 256:], left[1]))[64:]

def output_kernel(scale, mine, mine_proj, mine_update, got, right, member, out, update):
    proj = mine_proj[...] + unpaired(got[:ROWS, IN_BLOCK:])
    factor = lax.broadcasted_iota(jnp.int32, (ROWS, 128), 1) // RANK
    coefficient = jnp.where(member[...] == factor, proj, 0.0)[:, :32] * scale
    low_rank = jnp.dot(
        coefficient, right[...], precision=lax.Precision.HIGHEST, preferred_element_type=F32
    )
    out[...] = mine[...] + got[:ROWS, :IN_BLOCK].astype(F32) + low_rank
    update[...] = mine_update[...] + take_pair(got, ROWS)


def finish(mine, mine_proj, mine_update, got, right_local, member_of):
    vmem = pl.BlockSpec(memory_space=pltpu.VMEM)
    return pl.pallas_call(
        functools.partial(output_kernel, perturb_scale / math.sqrt(RANK)),
        out_shape=(
            jax.ShapeDtypeStruct((ROWS, IN_BLOCK), F32),
            jax.ShapeDtypeStruct((OUT_BLOCK, IN_BLOCK), F32),
        ),
        in_specs=[vmem] * 6,
        out_specs=(vmem, vmem),
        compiler_params=pltpu.CompilerParams(vmem_limit_bytes=56 * 2**20),
        cost_estimate=pl.CostEstimate(
            flops=12 * ROWS * 32 * IN_BLOCK, bytes_accessed=3 * 2**20, transcendentals=0
        ),
    )(mine, mine_proj, mine_update, got, right_local, member_of.reshape(ROWS, 1))


def on_device(tokens, base_weight, left_factors, right_factors, member_of, ranks):
    z, xl, core, y, xh = (lax.axis_index(name) for name in AXES)
    members = M_DEV * 64
    left = left_factors.astype(BF16).reshape(32, IN_BLOCK)
    offset = (y * 2 + xh) * IN_BLOCK
    right_local = lax.dynamic_slice_in_dim(right_factors, offset, IN_BLOCK, 2).reshape(32, IN_BLOCK)
    slot = jnp.concatenate([move(base_weight.T.astype(BF16), weight_target), left])
    slots = lax.all_gather(slot, "z", axis=0, tiled=True)
    rows = spread_rows(tokens, left, slot)
    right = spread_right(right_local, ranks, slot, z)

    place = jnp.stack([z, core, xl ^ xh, y, xh, xl]).astype(jnp.int32)
    total, proj, keep, give = main(place, members, slots, *rows, right)
    mine, mine_proj, mine_update, give = join(place, total, proj, keep, move(give, core_target))
    got = move(give, xl_target)
    outputs, update = finish(mine, mine_proj, mine_update, got, right_local, member_of)
    return (outputs, update.T)


def solution(mesh):
    fine = Mesh(mesh.devices.reshape(tuple(SIZES.values())), AXES)
    return jax.shard_map(
        on_device,
        mesh=fine,
        in_specs=(
            P(POP, TENSOR),
            P(TENSOR, POP),
            P(POP, None, TENSOR),
            P(POP, None, None),
            P(POP, None),
            P(POP),
        ),
        out_specs=(P(POP, TENSOR), P(TENSOR, POP)),
        check_vma=False,
    )
```

```python
import functools
import itertools
import math

import jax
import jax.numpy as jnp
from jax import lax
from jax.experimental import pallas as pl
from jax.experimental.pallas import tpu as pltpu
from jax.sharding import Mesh
from jax.sharding import PartitionSpec as P

D = 5120
RANK = 4
M_DEV = 8
ROWS = 192
IN_BLOCK = 640
OUT_BLOCK = 80
EXTRA = 80
SLOT = OUT_BLOCK + 32
GROUP_ROWS = 768
GIVE = 176

perturb_scale = 0.5

SIZES = {"z": 16, "xl": 2, "core": 2, "y": 4, "xh": 2}
AXES = tuple(SIZES)
POP = ("z", "xl", "core")
TENSOR = ("y", "xh")
BF16 = jnp.bfloat16
F32 = jnp.float32


def flat(place):
    index = 0
    for value, size in zip(place, SIZES.values()):
        index = index * size + value % size
    return index


def move(value, target):
    places = itertools.product(*(range(n) for n in SIZES.values()))
    return lax.ppermute(value, AXES, [(flat(p), flat(target(*p))) for p in places])


def right_target(near, z, xl, core, y, xh):
    return (z + 2 * (2 * y + xh) + near, xl, core, y, xh)


def core_target(z, xl, core, y, xh):
    return (z, xl, 1 - core, y, xh)


def xl_target(z, xl, core, y, xh):
    return (z, 1 - xl, core, y, xh)


def xh_target(z, xl, core, y, xh):
    return (z, xl, core, y, 1 - xh)


def y_pair_target(z, xl, core, y, xh):
    return (z, xl, core, y ^ 1, xh)


def y_half_target(z, xl, core, y, xh):
    return (z, xl, core, y + 2, xh)


def diagonal_target(z, xl, core, y, xh):
    return (z, 1 - xl, 1 - core, y, xh)


def nt_dot(a, b):
    return lax.dot_general(a, b, (((1,), (1,)), ((), ())), preferred_element_type=F32)


def split(value):
    high = lax.reduce_precision(value, 8, 7)
    return high.astype(BF16), (value - high).astype(BF16)


def product_kernel(place, slots, rows, left, member, give, weights):
    for source in range(16):
        block = slots[source * SLOT : source * SLOT + OUT_BLOCK, :]
        weights[source * OUT_BLOCK : (source + 1) * OUT_BLOCK, :] = block
    proj = nt_dot(left[...], rows[:ROWS, :])
    owner = lax.broadcasted_iota(jnp.int32, (32, ROWS), 0) // RANK
    proj = jnp.where(owner == member[...], proj, 0.0)
    folded = proj[:8] + proj[8:16] + proj[16:24] + proj[24:]
    high = folded.astype(BF16).astype(F32)
    pair = jnp.concatenate([high, folded - high]).astype(BF16)
    for part in range(2):
        block = nt_dot(weights[part * 640 : part * 640 + 640, :], rows[...])
        for i in range(4):
            at = part * 4 + i
            give[at, :160, :] = block[i * 160 : (i + 1) * 160].astype(BF16)
            give[at, 160:, :] = jnp.zeros((16, GROUP_ROWS), BF16)
            give[at, 160:, :ROWS] = pair


VMEM = pl.BlockSpec(memory_space=pltpu.VMEM)
SMEM = pl.BlockSpec(memory_space=pltpu.SMEM)
LIMIT = pltpu.CompilerParams(vmem_limit_bytes=50 * 2**20)


def shape(*dims, dtype=F32):
    return jax.ShapeDtypeStruct(dims, dtype)


def call(kernel, outs, place, arrays, scratch=(), flops=10**6, moved=4 * 2**20):
    return pl.pallas_call(
        kernel,
        out_shape=outs,
        in_specs=[SMEM] + [VMEM] * len(arrays),
        out_specs=(VMEM,) * len(outs),
        scratch_shapes=list(scratch),
        compiler_params=LIMIT,
        cost_estimate=pl.CostEstimate(flops=flops, bytes_accessed=moved, transcendentals=0),
    )(place, *arrays)


def update_kernel(members, place, slots, right, keep, give, total, *scratch):
    core = place[1]
    update_sums(members, place, slots, right, total, *scratch)
    for i in range(2):
        at = slice(i * OUT_BLOCK, (i + 1) * OUT_BLOCK)
        here = pl.ds(pl.multiple_of((2 * i + core) * OUT_BLOCK, 8), OUT_BLOCK)
        there = pl.ds(pl.multiple_of((2 * i + 1 - core) * OUT_BLOCK, 8), OUT_BLOCK)
        keep[at, :] = total[here, :]
        give[at, :] = total[there, :]


def join_kernel(place, keep, got, mine, give):
    xl = place[5]
    first = keep[:OUT_BLOCK, :] + got[:OUT_BLOCK, :]
    second = keep[OUT_BLOCK:, :] + got[OUT_BLOCK:, :]
    mine[...] = jnp.where(xl == 0, first, second)
    give[...] = jnp.where(xl == 0, second, first)


def sum_kernel(place, got, mine, coefficient, to_core, to_xl, to_diagonal):
    total, folded = 0.0, 0.0
    for index in range(8):
        total = total + got[index, :160, :].astype(F32)
        pair = got[index, 160:, :256].astype(F32)[:, :ROWS]
        folded = folded + pair[:8] + pair[8:]
    coefficient[...] = folded
    mine[...] = total[:, :256]
    to_core[...] = total[:, 384:640]
    to_xl[...] = pltpu.roll(total[:, :384], 192, 1)[:, :256].astype(BF16)
    to_diagonal[...] = pltpu.roll(total[:, 384:], 192, 1)[:, :256].astype(BF16)


def finish_kernel(
    scale, place, mine, from_core, from_xl, from_diagonal, coefficient, right, member, out, full
):
    core, xl = place[1], place[5]
    sources = (
        (mine, xl, core),
        (from_core, xl, 1 - core),
        (from_xl, 1 - xl, core),
        (from_diagonal, 1 - xl, 1 - core),
    )
    for ref, side, half in sources:
        for j in range(2):
            start = (4 * j + 2 * side + half) * OUT_BLOCK
            block = ref[j * OUT_BLOCK : (j + 1) * OUT_BLOCK, :].astype(F32)
            full[pl.ds(pl.multiple_of(start, 8), OUT_BLOCK), :] = block
    owner = lax.broadcasted_iota(jnp.int32, (32, ROWS), 0) // RANK
    factor = jnp.where(owner == member[...], jnp.concatenate([coefficient[...]] * 4), 0.0) * scale
    low_rank = lax.dot_general(
        factor,
        right[...],
        (((0,), (0,)), ((), ())),
        precision=lax.Precision.HIGHEST,
        preferred_element_type=F32,
    )
    out[...] = full[...].T[:ROWS] + low_rank


def zero_after(value):
    return jnp.where(value[-1, -1] == value[-1, -1], 0, 1).astype(jnp.int32)


def rank_row(ranks):
    own = jnp.pad(ranks.astype(BF16)[None, :], ((0, 15), (0, 120)))
    every = lax.all_gather(own, ("xl", "core"), axis=1, tiled=True)
    every = jnp.concatenate([every[:, g * 128 : g * 128 + M_DEV] for g in range(4)], 1)
    return jnp.pad(every, ((0, 0), (0, 320 - 4 * M_DEV)))


def spread_right(right_factors, ranks, z, tensor):
    levels = rank_row(ranks)
    parts = []
    for near in range(2):
        start = lax.rem(z + 2 * tensor + near, 16) * 320
        chunk = lax.dynamic_slice_in_dim(right_factors, start, 320, 2).reshape(32, 320)
        sent = jnp.concatenate([*split(chunk), levels])
        parts.append(jnp.pad(move(sent, functools.partial(right_target, near)), ((0, 0), (0, 64))))
    return jnp.concatenate(parts, 1)


def gather_right(held):
    for target in (xh_target, y_pair_target, y_half_target):
        held = jnp.concatenate([held, move(held, target)])
    return held


def update_sums(members, place, slots, right, total, left, high, low):
    z, core, y, xh, xl = place[0], place[1], place[3], place[4], place[5]
    blocks = [(far, pair, h) for far in range(2) for pair in range(2) for h in range(2)]
    lane = lax.broadcasted_iota(jnp.int32, (1, 128), 1)
    levels, spread, rank_sum = [], 0.0, 0.0
    for index in range(8):
        row = right[index * EXTRA + 64 : (index + 1) * EXTRA, :].astype(F32)[:1, :]
        levels.append([row[:, :128], row[:, 384:512]])
    for value in sum(levels, []):
        rank_sum = rank_sum + jnp.where(lane < 4 * M_DEV, value, 0.0)
    rank_mean = jnp.sum(rank_sum) / members
    for value in sum(levels, []):
        spread = spread + jnp.where(lane < 4 * M_DEV, (value - rank_mean) ** 2, 0.0)
    variance = jnp.full((8, 128), jnp.sum(spread) / members)
    scale = lax.rsqrt(variance + 1e-05)[:1, :1] * math.sqrt(D / (members * RANK))

    lane = lax.broadcasted_iota(jnp.int32, (32, 128), 1)
    member = lax.broadcasted_iota(jnp.int32, (32, 128), 0) // RANK + M_DEV * (2 * xl + core)
    in_first = lax.broadcasted_iota(jnp.int32, (32, GROUP_ROWS), 1) < 384
    for index, (far, pair, h) in enumerate(blocks):
        base = index * EXTRA
        rows = slice(index * 32, index * 32 + 32)
        level = [
            jnp.sum(jnp.where(lane == member, value, 0.0), axis=1, keepdims=True)
            for value in levels[index]
        ]
        fitness = (jnp.where(in_first, level[0], level[1]) - rank_mean) * scale
        scaled = fitness * (
            right[base : base + 32, :].astype(F32) + right[base + 32 : base + 64, :].astype(F32)
        )
        part = scaled.astype(BF16)
        high[rows, :] = part
        low[rows, :] = (scaled - part.astype(F32)).astype(BF16)
        owner = 2 * lax.rem((y ^ pair) + 2 * far, 4) + (xh ^ h)
        for near in range(2):
            start = lax.rem(z + 32 - 2 * owner - near, 16) * SLOT + OUT_BLOCK
            left[near, rows, :] = slots[pl.ds(pl.multiple_of(start, 16), 32), :]

    def tn_dot(a, b):
        return lax.dot_general(a, b, (((0,), (0,)), ((), ())), preferred_element_type=F32)

    for near in range(2):
        lanes = slice(near * 384, near * 384 + 384)
        part = (tn_dot(high[:, lanes], left[near]) + tn_dot(low[:, lanes], left[near]))[:320]
        total[...] = part if near == 0 else total[...] + part


def on_device(tokens, base_weight, left_factors, right_factors, member_of, ranks):
    z, xl, core, y, xh = (lax.axis_index(name) for name in AXES)
    members = M_DEV * 64
    left = left_factors.astype(BF16).reshape(32, IN_BLOCK)
    tensor = y * 2 + xh
    place = jnp.stack([z, core, xl ^ xh, y, xh, xl, tensor]).astype(jnp.int32)
    slot = jnp.concatenate([base_weight.T.astype(BF16), left])
    slots = lax.all_gather(slot, "z", axis=0, tiled=True)

    rows = jnp.concatenate([tokens, move(tokens, xl_target)])
    rows = jnp.concatenate([rows, move(rows, core_target)])
    right = gather_right(spread_right(right_factors, ranks, z, tensor))
    keep, give = call(
        functools.partial(update_kernel, members),
        (shape(160, IN_BLOCK), shape(160, IN_BLOCK)),
        place,
        (slots, right),
        [
            pltpu.VMEM((320, IN_BLOCK), F32),
            pltpu.VMEM((2, 256, IN_BLOCK), BF16),
            pltpu.VMEM((256, GROUP_ROWS), BF16),
            pltpu.VMEM((256, GROUP_ROWS), BF16),
        ],
        flops=8 * 384 * 256 * 640,
    )
    keep, give = call(
        join_kernel,
        (shape(OUT_BLOCK, IN_BLOCK), shape(OUT_BLOCK, IN_BLOCK)),
        place,
        (keep, move(give, core_target)),
    )
    update = keep + move(give, xl_target)

    (give,) = call(
        product_kernel,
        (shape(8, GIVE, GROUP_ROWS, dtype=BF16),),
        place + zero_after(right),
        (slots, rows, left, member_of),
        [pltpu.VMEM((2 * IN_BLOCK, IN_BLOCK), BF16)],
        flops=2 * 768 * 640 * 1280,
        moved=6 * 2**20,
    )
    got = lax.all_to_all(give, TENSOR, split_axis=0, concat_axis=0, tiled=True)
    block = (160, 256)
    mine, coefficient, to_core, to_xl, to_diagonal = call(
        sum_kernel,
        (shape(*block), shape(8, ROWS), shape(*block))
        + (shape(*block, dtype=BF16), shape(*block, dtype=BF16)),
        place,
        (got,),
    )
    right_local = lax.dynamic_slice_in_dim(right_factors, tensor * IN_BLOCK, IN_BLOCK, 2)
    (outputs,) = call(
        functools.partial(finish_kernel, perturb_scale / math.sqrt(RANK)),
        (shape(ROWS, IN_BLOCK),),
        place,
        (
            mine,
            move(to_core, core_target),
            move(to_xl, xl_target),
            move(to_diagonal, diagonal_target),
            coefficient,
            right_local.reshape(32, IN_BLOCK),
            member_of,
        ),
        [pltpu.VMEM((IN_BLOCK, 256), F32)],
        flops=12 * ROWS * 32 * IN_BLOCK,
    )
    return (outputs, update.T)


def solution(mesh):
    fine = Mesh(mesh.devices.reshape(tuple(SIZES.values())), AXES)
    return jax.shard_map(
        on_device,
        mesh=fine,
        in_specs=(
            P(POP, TENSOR),
            P(TENSOR, POP),
            P(POP, None, TENSOR),
            P(POP, None, None),
            P(POP, None),
            P(POP),
        ),
        out_specs=(P(POP, TENSOR), P(TENSOR, POP)),
        check_vma=False,
    )
```

```python
import functools
import itertools
import math

import jax
import jax.numpy as jnp
from jax import lax
from jax.experimental import pallas as pl
from jax.experimental.pallas import tpu as pltpu
from jax.sharding import Mesh
from jax.sharding import PartitionSpec as P

D = 5120
RANK = 4
M_DEV = 8
ROWS = 192
IN_BLOCK = 640
OUT_BLOCK = 80
EXTRA = 80
SLOT = OUT_BLOCK + 32
GROUP_ROWS = 768
GIVE = 176

perturb_scale = 0.5

SIZES = {"z": 16, "xl": 2, "core": 2, "y": 4, "xh": 2}
AXES = tuple(SIZES)
POP = ("z", "xl", "core")
TENSOR = ("y", "xh")
BF16 = jnp.bfloat16
F32 = jnp.float32


def flat(place):
    index = 0
    for value, size in zip(place, SIZES.values()):
        index = index * size + value % size
    return index


def move(value, target):
    places = itertools.product(*(range(n) for n in SIZES.values()))
    return lax.ppermute(value, AXES, [(flat(p), flat(target(*p))) for p in places])


def right_target(near, z, xl, core, y, xh):
    return (z + 2 * (2 * y + xh) + near, xl, core, y, xh)


def core_target(z, xl, core, y, xh):
    return (z, xl, 1 - core, y, xh)


def xl_target(z, xl, core, y, xh):
    return (z, 1 - xl, core, y, xh)


def half_target(z, xl, core, y, xh):
    half = z // 2 % 2
    return (z, xl, core, y, xh) if xh == half else (z ^ 2, xl, core, y, half)


def xh_target(z, xl, core, y, xh):
    return (z, xl, core, y, 1 - xh)


def y_pair_target(z, xl, core, y, xh):
    return (z, xl, core, y ^ 1, xh)


def y_half_target(z, xl, core, y, xh):
    return (z, xl, core, y + 2, xh)


def diagonal_target(z, xl, core, y, xh):
    return (z, 1 - xl, 1 - core, y, xh)


def nt_dot(a, b):
    return lax.dot_general(a, b, (((1,), (1,)), ((), ())), preferred_element_type=F32)


def split(value):
    high = lax.reduce_precision(value, 8, 7)
    return high.astype(BF16), (value - high).astype(BF16)


def product_kernel(place, slots, rows, left, other_left, member, give, weights, inputs):
    xh = place[4]
    for block in range(8):
        for other in range(2):
            source = 4 * (block // 2) + 2 * (xh ^ other) + block % 2
            start = pl.multiple_of(source * SLOT, 16)
            at = slice(block * OUT_BLOCK, (block + 1) * OUT_BLOCK)
            weights[other, at, :] = slots[pl.ds(start, OUT_BLOCK), :]
    for group in range(4):
        for other in range(2):
            at = slice(group * ROWS, (group + 1) * ROWS)
            start = (2 * group + other) * ROWS
            inputs[other, at, :] = rows[start : start + ROWS, :]

    proj = nt_dot(left[...], rows[:ROWS, :]) + nt_dot(other_left[...], rows[ROWS : 2 * ROWS, :])
    owner = lax.broadcasted_iota(jnp.int32, (32, ROWS), 0) // RANK
    proj = jnp.where(owner == member[...], proj, 0.0)
    folded = proj[:8] + proj[8:16] + proj[16:24] + proj[24:]
    high = folded.astype(BF16).astype(F32)
    pair = jnp.concatenate([high, folded - high]).astype(BF16)
    block = nt_dot(weights[0], inputs[0]) + nt_dot(weights[1], inputs[1])
    for at in range(4):
        give[at, :160, :] = block[at * 160 : (at + 1) * 160].astype(BF16)
        give[at, 160:, :] = jnp.zeros((16, GROUP_ROWS), BF16)
        give[at, 160:, :ROWS] = pair


VMEM = pl.BlockSpec(memory_space=pltpu.VMEM)
SMEM = pl.BlockSpec(memory_space=pltpu.SMEM)
LIMIT = pltpu.CompilerParams(vmem_limit_bytes=50 * 2**20)


def shape(*dims, dtype=F32):
    return jax.ShapeDtypeStruct(dims, dtype)


def call(kernel, outs, place, arrays, scratch=(), flops=10**6, moved=4 * 2**20):
    return pl.pallas_call(
        kernel,
        out_shape=outs,
        in_specs=[SMEM] + [VMEM] * len(arrays),
        out_specs=(VMEM,) * len(outs),
        scratch_shapes=list(scratch),
        compiler_params=LIMIT,
        cost_estimate=pl.CostEstimate(flops=flops, bytes_accessed=moved, transcendentals=0),
    )(place, *arrays)


def update_kernel(members, place, slots, right, keep, give, total, *scratch):
    core = place[1]
    update_sums(members, place, slots, right, total, *scratch)
    for i in range(2):
        at = slice(i * OUT_BLOCK, (i + 1) * OUT_BLOCK)
        here = pl.ds(pl.multiple_of((2 * i + core) * OUT_BLOCK, 8), OUT_BLOCK)
        there = pl.ds(pl.multiple_of((2 * i + 1 - core) * OUT_BLOCK, 8), OUT_BLOCK)
        keep[at, :] = total[here, :]
        give[at, :] = total[there, :]


def join_kernel(place, keep, got, mine, give):
    xl = place[5]
    first = keep[:OUT_BLOCK, :] + got[:OUT_BLOCK, :]
    second = keep[OUT_BLOCK:, :] + got[OUT_BLOCK:, :]
    mine[...] = jnp.where(xl == 0, first, second)
    give[...] = jnp.where(xl == 0, second, first)


def sum_kernel(place, got, mine, coefficient, to_core, to_xl, to_diagonal):
    total, folded = 0.0, 0.0
    for index in range(4):
        total = total + got[index, :160, :].astype(F32)
        pair = got[index, 160:, :256].astype(F32)[:, :ROWS]
        folded = folded + pair[:8] + pair[8:]
    coefficient[...] = folded
    mine[...] = total[:, :256]
    to_core[...] = total[:, 384:640]
    to_xl[...] = pltpu.roll(total[:, :384], 192, 1)[:, :256].astype(BF16)
    to_diagonal[...] = pltpu.roll(total[:, 384:], 192, 1)[:, :256].astype(BF16)


def finish_kernel(
    scale, place, mine, from_core, from_xl, from_diagonal, coefficient, right, member, out, full
):
    core, xl = place[1], place[5]
    sources = (
        (mine, xl, core),
        (from_core, xl, 1 - core),
        (from_xl, 1 - xl, core),
        (from_diagonal, 1 - xl, 1 - core),
    )
    for ref, side, half in sources:
        for j in range(2):
            start = (4 * j + 2 * side + half) * OUT_BLOCK
            block = ref[j * OUT_BLOCK : (j + 1) * OUT_BLOCK, :].astype(F32)
            full[pl.ds(pl.multiple_of(start, 8), OUT_BLOCK), :] = block
    owner = lax.broadcasted_iota(jnp.int32, (32, ROWS), 0) // RANK
    factor = jnp.where(owner == member[...], jnp.concatenate([coefficient[...]] * 4), 0.0) * scale
    low_rank = lax.dot_general(
        factor,
        right[...],
        (((0,), (0,)), ((), ())),
        precision=lax.Precision.HIGHEST,
        preferred_element_type=F32,
    )
    out[...] = full[...].T[:ROWS] + low_rank


def zero_after(value):
    return jnp.where(value[-1, -1] == value[-1, -1], 0, 1).astype(jnp.int32)


def rank_row(ranks):
    own = jnp.pad(ranks.astype(BF16)[None, :], ((0, 15), (0, 120)))
    every = lax.all_gather(own, ("xl", "core"), axis=1, tiled=True)
    every = jnp.concatenate([every[:, g * 128 : g * 128 + M_DEV] for g in range(4)], 1)
    return jnp.pad(every, ((0, 0), (0, 320 - 4 * M_DEV)))


def spread_right(right_factors, ranks, z, tensor):
    levels = rank_row(ranks)
    parts = []
    for near in range(2):
        start = lax.rem(z + 2 * tensor + near, 16) * 320
        chunk = lax.dynamic_slice_in_dim(right_factors, start, 320, 2).reshape(32, 320)
        sent = jnp.concatenate([*split(chunk), levels])
        parts.append(jnp.pad(move(sent, functools.partial(right_target, near)), ((0, 0), (0, 64))))
    return jnp.concatenate(parts, 1)


def gather_right(held):
    for target in (xh_target, y_pair_target, y_half_target):
        held = jnp.concatenate([held, move(held, target)])
    return held


def update_sums(members, place, slots, right, total, left, high, low):
    z, core, y, xh, xl = place[0], place[1], place[3], place[4], place[5]
    blocks = [(far, pair, h) for far in range(2) for pair in range(2) for h in range(2)]
    lane = lax.broadcasted_iota(jnp.int32, (1, 128), 1)
    levels, spread, rank_sum = [], 0.0, 0.0
    for index in range(8):
        row = right[index * EXTRA + 64 : (index + 1) * EXTRA, :].astype(F32)[:1, :]
        levels.append([row[:, :128], row[:, 384:512]])
    for value in sum(levels, []):
        rank_sum = rank_sum + jnp.where(lane < 4 * M_DEV, value, 0.0)
    rank_mean = jnp.sum(rank_sum) / members
    for value in sum(levels, []):
        spread = spread + jnp.where(lane < 4 * M_DEV, (value - rank_mean) ** 2, 0.0)
    variance = jnp.full((8, 128), jnp.sum(spread) / members)
    scale = lax.rsqrt(variance + 1e-05)[:1, :1] * math.sqrt(D / (members * RANK))

    lane = lax.broadcasted_iota(jnp.int32, (32, 128), 1)
    member = lax.broadcasted_iota(jnp.int32, (32, 128), 0) // RANK + M_DEV * (2 * xl + core)
    in_first = lax.broadcasted_iota(jnp.int32, (32, GROUP_ROWS), 1) < 384
    for index, (far, pair, h) in enumerate(blocks):
        base = index * EXTRA
        rows = slice(index * 32, index * 32 + 32)
        level = [
            jnp.sum(jnp.where(lane == member, value, 0.0), axis=1, keepdims=True)
            for value in levels[index]
        ]
        fitness = (jnp.where(in_first, level[0], level[1]) - rank_mean) * scale
        scaled = fitness * (
            right[base : base + 32, :].astype(F32) + right[base + 32 : base + 64, :].astype(F32)
        )
        part = scaled.astype(BF16)
        high[rows, :] = part
        low[rows, :] = (scaled - part.astype(F32)).astype(BF16)
        owner = 2 * lax.rem((y ^ pair) + 2 * far, 4) + (xh ^ h)
        for near in range(2):
            start = lax.rem(z + 32 - 2 * owner - near, 16) * SLOT + OUT_BLOCK
            left[near, rows, :] = slots[pl.ds(pl.multiple_of(start, 16), 32), :]

    def tn_dot(a, b):
        return lax.dot_general(a, b, (((0,), (0,)), ((), ())), preferred_element_type=F32)

    for near in range(2):
        lanes = slice(near * 384, near * 384 + 384)
        part = (tn_dot(high[:, lanes], left[near]) + tn_dot(low[:, lanes], left[near]))[:320]
        total[...] = part if near == 0 else total[...] + part


def on_device(tokens, base_weight, left_factors, right_factors, member_of, ranks):
    z, xl, core, y, xh = (lax.axis_index(name) for name in AXES)
    members = M_DEV * 64
    left = left_factors.astype(BF16).reshape(32, IN_BLOCK)
    tensor = y * 2 + xh
    place = jnp.stack([z, core, xl ^ xh, y, xh, xl, tensor]).astype(jnp.int32)
    slot = jnp.concatenate([move(base_weight.T.astype(BF16), half_target), left])
    slots = lax.all_gather(slot, "z", axis=0, tiled=True)

    other = move(jnp.concatenate([tokens, left]), xh_target)
    rows = jnp.concatenate([tokens, other[:ROWS]])
    rows = jnp.concatenate([rows, move(rows, xl_target)])
    rows = jnp.concatenate([rows, move(rows, core_target)])
    right = gather_right(spread_right(right_factors, ranks, z, tensor))
    keep, give = call(
        functools.partial(update_kernel, members),
        (shape(160, IN_BLOCK), shape(160, IN_BLOCK)),
        place,
        (slots, right),
        [
            pltpu.VMEM((320, IN_BLOCK), F32),
            pltpu.VMEM((2, 256, IN_BLOCK), BF16),
            pltpu.VMEM((256, GROUP_ROWS), BF16),
            pltpu.VMEM((256, GROUP_ROWS), BF16),
        ],
        flops=8 * 384 * 256 * 640,
    )
    keep, give = call(
        join_kernel,
        (shape(OUT_BLOCK, IN_BLOCK), shape(OUT_BLOCK, IN_BLOCK)),
        place,
        (keep, move(give, core_target)),
    )
    update = keep + move(give, xl_target)

    (give,) = call(
        product_kernel,
        (shape(4, GIVE, GROUP_ROWS, dtype=BF16),),
        place + zero_after(right),
        (slots, rows, left, other[ROWS:], member_of),
        [pltpu.VMEM((2, IN_BLOCK, IN_BLOCK), BF16), pltpu.VMEM((2, GROUP_ROWS, IN_BLOCK), BF16)],
        flops=2 * 768 * 640 * 1280,
        moved=6 * 2**20,
    )
    got = lax.all_to_all(give, "y", split_axis=0, concat_axis=0, tiled=True)
    block = (160, 256)
    mine, coefficient, to_core, to_xl, to_diagonal = call(
        sum_kernel,
        (shape(*block), shape(8, ROWS), shape(*block))
        + (shape(*block, dtype=BF16), shape(*block, dtype=BF16)),
        place,
        (got,),
    )
    right_local = lax.dynamic_slice_in_dim(right_factors, tensor * IN_BLOCK, IN_BLOCK, 2)
    (outputs,) = call(
        functools.partial(finish_kernel, perturb_scale / math.sqrt(RANK)),
        (shape(ROWS, IN_BLOCK),),
        place,
        (
            mine,
            move(to_core, core_target),
            move(to_xl, xl_target),
            move(to_diagonal, diagonal_target),
            coefficient,
            right_local.reshape(32, IN_BLOCK),
            member_of,
        ),
        [pltpu.VMEM((IN_BLOCK, 256), F32)],
        flops=12 * ROWS * 32 * IN_BLOCK,
    )
    return (outputs, update.T)


def solution(mesh):
    fine = Mesh(mesh.devices.reshape(tuple(SIZES.values())), AXES)
    return jax.shard_map(
        on_device,
        mesh=fine,
        in_specs=(
            P(POP, TENSOR),
            P(TENSOR, POP),
            P(POP, None, TENSOR),
            P(POP, None, None),
            P(POP, None),
            P(POP),
        ),
        out_specs=(P(POP, TENSOR), P(TENSOR, POP)),
        check_vma=False,
    )
```

```python
import functools
import itertools
import math

import jax
import jax.numpy as jnp
from jax import lax
from jax.experimental import pallas as pl
from jax.experimental.pallas import tpu as pltpu
from jax.sharding import Mesh
from jax.sharding import PartitionSpec as P

D = 5120
RANK = 4
M_DEV = 8
ROWS = 192
IN_BLOCK = 640
OUT_BLOCK = 80
EXTRA = 80
SLOT = OUT_BLOCK + 32
GROUP_ROWS = 768
GIVE = 176

perturb_scale = 0.5

SIZES = {"z": 16, "xl": 2, "core": 2, "y": 4, "xh": 2}
AXES = tuple(SIZES)
POP = ("z", "xl", "core")
TENSOR = ("y", "xh")
BF16 = jnp.bfloat16
F32 = jnp.float32


def flat(place):
    index = 0
    for value, size in zip(place, SIZES.values()):
        index = index * size + value % size
    return index


def move(value, target):
    places = itertools.product(*(range(n) for n in SIZES.values()))
    return lax.ppermute(value, AXES, [(flat(p), flat(target(*p))) for p in places])


def right_target(near, z, xl, core, y, xh):
    return (z + 2 * (2 * y + xh) + near, xl, core, y, xh)


def core_target(z, xl, core, y, xh):
    return (z, xl, 1 - core, y, xh)


def xl_target(z, xl, core, y, xh):
    return (z, 1 - xl, core, y, xh)


def half_target(z, xl, core, y, xh):
    half = z // 2 % 2
    return (z, xl, core, y, xh) if xh == half else (z ^ 2, xl, core, y, half)


def xh_target(z, xl, core, y, xh):
    return (z, xl, core, y, 1 - xh)


def y_pair_target(z, xl, core, y, xh):
    return (z, xl, core, y ^ 1, xh)


def y_half_target(z, xl, core, y, xh):
    return (z, xl, core, y + 2, xh)


def diagonal_target(z, xl, core, y, xh):
    return (z, 1 - xl, 1 - core, y, xh)


def nt_dot(a, b):
    return lax.dot_general(a, b, (((1,), (1,)), ((), ())), preferred_element_type=F32)


def split(value):
    high = lax.reduce_precision(value, 8, 7)
    return high.astype(BF16), (value - high).astype(BF16)


def product_kernel(place, slots, rows, left, other_left, member, give, weights, inputs):
    xh = place[4]
    for block in range(8):
        for other in range(2):
            source = 4 * (block // 2) + 2 * (xh ^ other) + block % 2
            start = pl.multiple_of(source * SLOT, 16)
            at = slice(block * OUT_BLOCK, (block + 1) * OUT_BLOCK)
            weights[other, at, :] = slots[pl.ds(start, OUT_BLOCK), :]
    for group in range(4):
        for other in range(2):
            at = slice(group * ROWS, (group + 1) * ROWS)
            start = (2 * group + other) * ROWS
            inputs[other, at, :] = rows[start : start + ROWS, :]

    proj = nt_dot(left[...], rows[:ROWS, :]) + nt_dot(other_left[...], rows[ROWS : 2 * ROWS, :])
    owner = lax.broadcasted_iota(jnp.int32, (32, ROWS), 0) // RANK
    proj = jnp.where(owner == member[...], proj, 0.0)
    folded = proj[:8] + proj[8:16] + proj[16:24] + proj[24:]
    high = folded.astype(BF16).astype(F32)
    pair = jnp.concatenate([high, folded - high]).astype(BF16)
    block = nt_dot(weights[0], inputs[0]) + nt_dot(weights[1], inputs[1])
    for at in range(4):
        give[at, :160, :] = block[at * 160 : (at + 1) * 160].astype(BF16)
        give[at, 160:, :] = jnp.zeros((16, GROUP_ROWS), BF16)
        give[at, 160:, :ROWS] = pair


VMEM = pl.BlockSpec(memory_space=pltpu.VMEM)
SMEM = pl.BlockSpec(memory_space=pltpu.SMEM)
LIMIT = pltpu.CompilerParams(vmem_limit_bytes=50 * 2**20)


def shape(*dims, dtype=F32):
    return jax.ShapeDtypeStruct(dims, dtype)


def call(kernel, outs, place, arrays, scratch=(), flops=10**6, moved=4 * 2**20):
    return pl.pallas_call(
        kernel,
        out_shape=outs,
        in_specs=[SMEM] + [VMEM] * len(arrays),
        out_specs=(VMEM,) * len(outs),
        scratch_shapes=list(scratch),
        compiler_params=LIMIT,
        cost_estimate=pl.CostEstimate(flops=flops, bytes_accessed=moved, transcendentals=0),
    )(place, *arrays)


def update_kernel(members, place, slots, right, keep, give, total, *scratch):
    core = place[1]
    update_sums(members, place, slots, right, total, *scratch)
    for i in range(2):
        at = slice(i * OUT_BLOCK, (i + 1) * OUT_BLOCK)
        here = pl.ds(pl.multiple_of((2 * i + core) * OUT_BLOCK, 8), OUT_BLOCK)
        there = pl.ds(pl.multiple_of((2 * i + 1 - core) * OUT_BLOCK, 8), OUT_BLOCK)
        keep[at, :] = total[here, :]
        give[at, :] = total[there, :]


def join_kernel(place, keep, got, mine, give):
    xl = place[5]
    first = keep[:OUT_BLOCK, :] + got[:OUT_BLOCK, :]
    second = keep[OUT_BLOCK:, :] + got[OUT_BLOCK:, :]
    mine[...] = jnp.where(xl == 0, first, second)
    give[...] = jnp.where(xl == 0, second, first)


def sum_kernel(place, got, mine, coefficient, to_core, to_xl, to_diagonal):
    total, folded = 0.0, 0.0
    for index in range(4):
        total = total + got[index, :160, :].astype(F32)
        pair = got[index, 160:, :256].astype(F32)[:, :ROWS]
        folded = folded + pair[:8] + pair[8:]
    coefficient[...] = folded
    mine[...] = total[:, :256]
    to_core[...] = total[:, 384:640]
    to_xl[...] = pltpu.roll(total[:, :384], 192, 1)[:, :256].astype(BF16)
    to_diagonal[...] = pltpu.roll(total[:, 384:], 192, 1)[:, :256].astype(BF16)


def finish_kernel(
    scale, place, mine, from_core, from_xl, from_diagonal, coefficient, right, member, out, full
):
    core, xl = place[1], place[5]
    sources = (
        (mine, xl, core),
        (from_core, xl, 1 - core),
        (from_xl, 1 - xl, core),
        (from_diagonal, 1 - xl, 1 - core),
    )
    for ref, side, half in sources:
        for j in range(2):
            start = (4 * j + 2 * side + half) * OUT_BLOCK
            block = ref[j * OUT_BLOCK : (j + 1) * OUT_BLOCK, :].astype(F32)
            full[pl.ds(pl.multiple_of(start, 8), OUT_BLOCK), :] = block
    owner = lax.broadcasted_iota(jnp.int32, (32, ROWS), 0) // RANK
    factor = jnp.where(owner == member[...], jnp.concatenate([coefficient[...]] * 4), 0.0) * scale
    low_rank = lax.dot_general(
        factor,
        right[...],
        (((0,), (0,)), ((), ())),
        precision=lax.Precision.HIGHEST,
        preferred_element_type=F32,
    )
    out[...] = full[...].T[:ROWS] + low_rank


def zero_after(value):
    return jnp.where(value[-1, -1] == value[-1, -1], 0, 1).astype(jnp.int32)


def rank_row(ranks):
    own = jnp.pad(ranks.astype(BF16)[None, :], ((0, 15), (0, 120)))
    every = lax.all_gather(own, ("xl", "core"), axis=1, tiled=True)
    every = jnp.concatenate([every[:, g * 128 : g * 128 + M_DEV] for g in range(4)], 1)
    return jnp.pad(every, ((0, 0), (0, 320 - 4 * M_DEV)))


def after(value, other):
    return jnp.where(other[0, 0] == other[0, 0], value, jnp.zeros_like(value))


def spread_right(right_factors, levels, z, tensor):
    parts = []
    for near in range(2):
        start = lax.rem(z + 2 * tensor + near, 16) * 320
        chunk = lax.dynamic_slice_in_dim(right_factors, start, 320, 2).reshape(32, 320)
        sent = jnp.concatenate([*split(chunk), levels])
        parts.append(jnp.pad(move(sent, functools.partial(right_target, near)), ((0, 0), (0, 64))))
    return jnp.concatenate(parts, 1)


def gather_right(held):
    for target in (xh_target, y_pair_target, y_half_target):
        held = jnp.concatenate([held, move(held, target)])
    return held


def update_sums(members, place, slots, right, total, left, high, low):
    z, core, y, xh, xl = place[0], place[1], place[3], place[4], place[5]
    blocks = [(far, pair, h) for far in range(2) for pair in range(2) for h in range(2)]
    lane = lax.broadcasted_iota(jnp.int32, (1, 128), 1)
    levels, spread, rank_sum = [], 0.0, 0.0
    for index in range(8):
        row = right[index * EXTRA + 64 : (index + 1) * EXTRA, :].astype(F32)[:1, :]
        levels.append([row[:, :128], row[:, 384:512]])
    for value in sum(levels, []):
        rank_sum = rank_sum + jnp.where(lane < 4 * M_DEV, value, 0.0)
    rank_mean = jnp.sum(rank_sum) / members
    for value in sum(levels, []):
        spread = spread + jnp.where(lane < 4 * M_DEV, (value - rank_mean) ** 2, 0.0)
    variance = jnp.full((8, 128), jnp.sum(spread) / members)
    scale = lax.rsqrt(variance + 1e-05)[:1, :1] * math.sqrt(D / (members * RANK))

    lane = lax.broadcasted_iota(jnp.int32, (32, 128), 1)
    member = lax.broadcasted_iota(jnp.int32, (32, 128), 0) // RANK + M_DEV * (2 * xl + core)
    in_first = lax.broadcasted_iota(jnp.int32, (32, GROUP_ROWS), 1) < 384
    for index, (far, pair, h) in enumerate(blocks):
        base = index * EXTRA
        rows = slice(index * 32, index * 32 + 32)
        level = [
            jnp.sum(jnp.where(lane == member, value, 0.0), axis=1, keepdims=True)
            for value in levels[index]
        ]
        fitness = (jnp.where(in_first, level[0], level[1]) - rank_mean) * scale
        scaled = fitness * (
            right[base : base + 32, :].astype(F32) + right[base + 32 : base + 64, :].astype(F32)
        )
        part = scaled.astype(BF16)
        high[rows, :] = part
        low[rows, :] = (scaled - part.astype(F32)).astype(BF16)
        owner = 2 * lax.rem((y ^ pair) + 2 * far, 4) + (xh ^ h)
        for near in range(2):
            start = lax.rem(z + 32 - 2 * owner - near, 16) * SLOT + OUT_BLOCK
            left[near, rows, :] = slots[pl.ds(pl.multiple_of(start, 16), 32), :]

    def tn_dot(a, b):
        return lax.dot_general(a, b, (((0,), (0,)), ((), ())), preferred_element_type=F32)

    for near in range(2):
        lanes = slice(near * 384, near * 384 + 384)
        part = (tn_dot(high[:, lanes], left[near]) + tn_dot(low[:, lanes], left[near]))[:320]
        total[...] = part if near == 0 else total[...] + part


def on_device(tokens, base_weight, left_factors, right_factors, member_of, ranks):
    z, xl, core, y, xh = (lax.axis_index(name) for name in AXES)
    members = M_DEV * 64
    left = left_factors.astype(BF16).reshape(32, IN_BLOCK)
    tensor = y * 2 + xh
    place = jnp.stack([z, core, xl ^ xh, y, xh, xl, tensor]).astype(jnp.int32)
    slot = jnp.concatenate([move(base_weight.T.astype(BF16), half_target), left])
    slots = lax.all_gather(slot, "z", axis=0, tiled=True)

    levels = rank_row(ranks)
    other = move(after(jnp.concatenate([tokens, left]), levels), xh_target)
    rows = jnp.concatenate([tokens, other[:ROWS]])
    rows = jnp.concatenate([rows, move(rows, xl_target)])
    rows = jnp.concatenate([rows, move(rows, core_target)])
    right = gather_right(spread_right(right_factors, levels, z, tensor))
    keep, give = call(
        functools.partial(update_kernel, members),
        (shape(160, IN_BLOCK), shape(160, IN_BLOCK)),
        place,
        (slots, right),
        [
            pltpu.VMEM((320, IN_BLOCK), F32),
            pltpu.VMEM((2, 256, IN_BLOCK), BF16),
            pltpu.VMEM((256, GROUP_ROWS), BF16),
            pltpu.VMEM((256, GROUP_ROWS), BF16),
        ],
        flops=8 * 384 * 256 * 640,
    )
    keep, give = call(
        join_kernel,
        (shape(OUT_BLOCK, IN_BLOCK), shape(OUT_BLOCK, IN_BLOCK)),
        place,
        (keep, move(give, core_target)),
    )
    update = keep + move(give, xl_target)

    (give,) = call(
        product_kernel,
        (shape(4, GIVE, GROUP_ROWS, dtype=BF16),),
        place + zero_after(right),
        (slots, rows, left, other[ROWS:], member_of),
        [pltpu.VMEM((2, IN_BLOCK, IN_BLOCK), BF16), pltpu.VMEM((2, GROUP_ROWS, IN_BLOCK), BF16)],
        flops=2 * 768 * 640 * 1280,
        moved=6 * 2**20,
    )
    got = lax.all_to_all(give, "y", split_axis=0, concat_axis=0, tiled=True)
    block = (160, 256)
    mine, coefficient, to_core, to_xl, to_diagonal = call(
        sum_kernel,
        (shape(*block), shape(8, ROWS), shape(*block))
        + (shape(*block, dtype=BF16), shape(*block, dtype=BF16)),
        place,
        (got,),
    )
    right_local = lax.dynamic_slice_in_dim(right_factors, tensor * IN_BLOCK, IN_BLOCK, 2)
    (outputs,) = call(
        functools.partial(finish_kernel, perturb_scale / math.sqrt(RANK)),
        (shape(ROWS, IN_BLOCK),),
        place,
        (
            mine,
            move(to_core, core_target),
            move(to_xl, xl_target),
            move(to_diagonal, diagonal_target),
            coefficient,
            right_local.reshape(32, IN_BLOCK),
            member_of,
        ),
        [pltpu.VMEM((IN_BLOCK, 256), F32)],
        flops=12 * ROWS * 32 * IN_BLOCK,
    )
    return (outputs, update.T)


def solution(mesh):
    fine = Mesh(mesh.devices.reshape(tuple(SIZES.values())), AXES)
    return jax.shard_map(
        on_device,
        mesh=fine,
        in_specs=(
            P(POP, TENSOR),
            P(TENSOR, POP),
            P(POP, None, TENSOR),
            P(POP, None, None),
            P(POP, None),
            P(POP),
        ),
        out_specs=(P(POP, TENSOR), P(TENSOR, POP)),
        check_vma=False,
    )
```

```python
import functools
import itertools
import math

import jax
import jax.numpy as jnp
from jax import lax
from jax.experimental import pallas as pl
from jax.experimental.pallas import tpu as pltpu
from jax.sharding import Mesh
from jax.sharding import PartitionSpec as P

D = 5120
RANK = 4
M_DEV = 8
ROWS = 192
IN_BLOCK = 640
OUT_BLOCK = 80
EXTRA = 80
SLOT = OUT_BLOCK + 32
GROUP_ROWS = 768
GIVE = 176

perturb_scale = 0.5

SIZES = {"z": 16, "xl": 2, "core": 2, "y": 4, "xh": 2}
AXES = tuple(SIZES)
POP = ("z", "xl", "core")
TENSOR = ("y", "xh")
BF16 = jnp.bfloat16
F32 = jnp.float32


def flat(place):
    index = 0
    for value, size in zip(place, SIZES.values()):
        index = index * size + value % size
    return index


def move(value, target):
    places = itertools.product(*(range(n) for n in SIZES.values()))
    return lax.ppermute(value, AXES, [(flat(p), flat(target(*p))) for p in places])


def right_target(near, z, xl, core, y, xh):
    return (z + 2 * (2 * y + xh) + near, xl, core, y, xh)


def core_target(z, xl, core, y, xh):
    return (z, xl, 1 - core, y, xh)


def xl_target(z, xl, core, y, xh):
    return (z, 1 - xl, core, y, xh)


def half_target(z, xl, core, y, xh):
    half = z // 2 % 2
    return (z, xl, core, y, xh) if xh == half else (z ^ 2, xl, core, y, half)


def xh_target(z, xl, core, y, xh):
    return (z, xl, core, y, 1 - xh)


def y_pair_target(z, xl, core, y, xh):
    return (z, xl, core, y ^ 1, xh)


def y_half_target(z, xl, core, y, xh):
    return (z, xl, core, y + 2, xh)


def diagonal_target(z, xl, core, y, xh):
    return (z, 1 - xl, 1 - core, y, xh)


def nt_dot(a, b):
    return lax.dot_general(a, b, (((1,), (1,)), ((), ())), preferred_element_type=F32)


def split(value):
    high = lax.reduce_precision(value, 8, 7)
    return high.astype(BF16), (value - high).astype(BF16)


def product_kernel(place, slots, rows, left, other_left, member, give, weights, inputs):
    xh = place[4]
    for block in range(8):
        for other in range(2):
            source = 4 * (block // 2) + 2 * (xh ^ other) + block % 2
            start = pl.multiple_of(source * SLOT, 16)
            at = slice(block * OUT_BLOCK, (block + 1) * OUT_BLOCK)
            weights[other, at, :] = slots[pl.ds(start, OUT_BLOCK), :]
    for group in range(4):
        for other in range(2):
            at = slice(group * ROWS, (group + 1) * ROWS)
            start = (2 * group + other) * ROWS
            inputs[other, at, :] = rows[start : start + ROWS, :]

    proj = nt_dot(left[...], rows[:ROWS, :]) + nt_dot(other_left[...], rows[ROWS : 2 * ROWS, :])
    owner = lax.broadcasted_iota(jnp.int32, (32, ROWS), 0) // RANK
    proj = jnp.where(owner == member[...], proj, 0.0)
    folded = proj[:8] + proj[8:16] + proj[16:24] + proj[24:]
    high = folded.astype(BF16).astype(F32)
    pair = jnp.concatenate([high, folded - high]).astype(BF16)
    block = nt_dot(weights[0], inputs[0]) + nt_dot(weights[1], inputs[1])
    for at in range(4):
        give[at, :160, :] = block[at * 160 : (at + 1) * 160].astype(BF16)
        give[at, 160:, :] = jnp.zeros((16, GROUP_ROWS), BF16)
        give[at, 160:, :ROWS] = pair


VMEM = pl.BlockSpec(memory_space=pltpu.VMEM)
SMEM = pl.BlockSpec(memory_space=pltpu.SMEM)
LIMIT = pltpu.CompilerParams(vmem_limit_bytes=50 * 2**20)


def shape(*dims, dtype=F32):
    return jax.ShapeDtypeStruct(dims, dtype)


def call(kernel, outs, place, arrays, scratch=(), flops=10**6, moved=4 * 2**20):
    return pl.pallas_call(
        kernel,
        out_shape=outs,
        in_specs=[SMEM] + [VMEM] * len(arrays),
        out_specs=(VMEM,) * len(outs),
        scratch_shapes=list(scratch),
        compiler_params=LIMIT,
        cost_estimate=pl.CostEstimate(flops=flops, bytes_accessed=moved, transcendentals=0),
    )(place, *arrays)


def update_kernel(members, place, slots, right, keep, give, total, *scratch):
    core = place[1]
    update_sums(members, place, slots, right, total, *scratch)
    for i in range(2):
        at = slice(i * OUT_BLOCK, (i + 1) * OUT_BLOCK)
        here = pl.ds(pl.multiple_of((2 * i + core) * OUT_BLOCK, 8), OUT_BLOCK)
        there = pl.ds(pl.multiple_of((2 * i + 1 - core) * OUT_BLOCK, 8), OUT_BLOCK)
        keep[at, :] = total[here, :]
        give[at, :] = total[there, :]


def join_kernel(place, keep, got, mine, give):
    xl = place[5]
    first = keep[:OUT_BLOCK, :] + got[:OUT_BLOCK, :]
    second = keep[OUT_BLOCK:, :] + got[OUT_BLOCK:, :]
    mine[...] = jnp.where(xl == 0, first, second)
    give[...] = jnp.where(xl == 0, second, first)


def sum_kernel(place, got, mine, coefficient, to_core, to_xl, to_diagonal):
    total, folded = 0.0, 0.0
    for index in range(4):
        total = total + got[index, :160, :].astype(F32)
        pair = got[index, 160:, :256].astype(F32)[:, :ROWS]
        folded = folded + pair[:8] + pair[8:]
    coefficient[...] = folded
    mine[...] = total[:, :256]
    to_core[...] = total[:, 384:640]
    to_xl[...] = pltpu.roll(total[:, :384], 192, 1)[:, :256].astype(BF16)
    to_diagonal[...] = pltpu.roll(total[:, 384:], 192, 1)[:, :256].astype(BF16)


def finish_kernel(
    scale, place, mine, from_core, from_xl, from_diagonal, coefficient, right, member, out, full
):
    core, xl = place[1], place[5]
    sources = (
        (mine, xl, core),
        (from_core, xl, 1 - core),
        (from_xl, 1 - xl, core),
        (from_diagonal, 1 - xl, 1 - core),
    )
    for ref, side, half in sources:
        for j in range(2):
            start = (4 * j + 2 * side + half) * OUT_BLOCK
            block = ref[j * OUT_BLOCK : (j + 1) * OUT_BLOCK, :].astype(F32)
            full[pl.ds(pl.multiple_of(start, 8), OUT_BLOCK), :] = block
    owner = lax.broadcasted_iota(jnp.int32, (32, ROWS), 0) // RANK
    factor = jnp.where(owner == member[...], jnp.concatenate([coefficient[...]] * 4), 0.0) * scale
    low_rank = lax.dot_general(
        factor,
        right[...],
        (((0,), (0,)), ((), ())),
        precision=lax.Precision.HIGHEST,
        preferred_element_type=F32,
    )
    out[...] = full[...].T[:ROWS] + low_rank


def zero_after(value):
    return jnp.where(value[-1, -1] == value[-1, -1], 0, 1).astype(jnp.int32)


def rank_row(ranks):
    own = jnp.pad(ranks.astype(BF16)[None, :], ((0, 15), (0, 120)))
    every = lax.all_gather(own, ("xl", "core"), axis=1, tiled=True)
    every = jnp.concatenate([every[:, g * 128 : g * 128 + M_DEV] for g in range(4)], 1)
    return jnp.pad(every, ((0, 0), (0, 320 - 4 * M_DEV)))


def after(value, other):
    return jnp.where(other[0, 0] == other[0, 0], value, jnp.zeros_like(value))


def spread_right(right_factors, levels, z, tensor):
    parts = []
    for near in range(2):
        start = lax.rem(z + 2 * tensor + near, 16) * 320
        chunk = lax.dynamic_slice_in_dim(right_factors, start, 320, 2).reshape(32, 320)
        sent = jnp.concatenate([*split(chunk), levels])
        parts.append(jnp.pad(move(sent, functools.partial(right_target, near)), ((0, 0), (0, 64))))
    return jnp.concatenate(parts, 1)


def gather_right(held):
    for target in (xh_target, y_pair_target, y_half_target):
        held = jnp.concatenate([held, move(held, target)])
    return held


def update_sums(members, place, slots, right, total, left, high, low):
    z, core, y, xh, xl = place[0], place[1], place[3], place[4], place[5]
    blocks = [(far, pair, h) for far in range(2) for pair in range(2) for h in range(2)]
    lane = lax.broadcasted_iota(jnp.int32, (1, 128), 1)
    levels, spread, rank_sum = [], 0.0, 0.0
    for index in range(8):
        row = right[index * EXTRA + 64 : (index + 1) * EXTRA, :].astype(F32)[:1, :]
        levels.append([row[:, :128], row[:, 384:512]])
    for value in sum(levels, []):
        rank_sum = rank_sum + jnp.where(lane < 4 * M_DEV, value, 0.0)
    rank_mean = jnp.sum(rank_sum) / members
    for value in sum(levels, []):
        spread = spread + jnp.where(lane < 4 * M_DEV, (value - rank_mean) ** 2, 0.0)
    variance = jnp.full((8, 128), jnp.sum(spread) / members)
    scale = lax.rsqrt(variance + 1e-05)[:1, :1] * math.sqrt(D / (members * RANK))

    lane = lax.broadcasted_iota(jnp.int32, (32, 128), 1)
    member = lax.broadcasted_iota(jnp.int32, (32, 128), 0) // RANK + M_DEV * (2 * xl + core)
    in_first = lax.broadcasted_iota(jnp.int32, (32, GROUP_ROWS), 1) < 384
    for index, (far, pair, h) in enumerate(blocks):
        base = index * EXTRA
        rows = slice(index * 32, index * 32 + 32)
        level = [
            jnp.sum(jnp.where(lane == member, value, 0.0), axis=1, keepdims=True)
            for value in levels[index]
        ]
        fitness = (jnp.where(in_first, level[0], level[1]) - rank_mean) * scale
        scaled = fitness * (
            right[base : base + 32, :].astype(F32) + right[base + 32 : base + 64, :].astype(F32)
        )
        part = scaled.astype(BF16)
        high[rows, :] = part
        low[rows, :] = (scaled - part.astype(F32)).astype(BF16)
        owner = 2 * lax.rem((y ^ pair) + 2 * far, 4) + (xh ^ h)
        for near in range(2):
            start = lax.rem(z + 32 - 2 * owner - near, 16) * SLOT + OUT_BLOCK
            left[near, rows, :] = slots[pl.ds(pl.multiple_of(start, 16), 32), :]

    def tn_dot(a, b):
        return lax.dot_general(a, b, (((0,), (0,)), ((), ())), preferred_element_type=F32)

    for near in range(2):
        lanes = slice(near * 384, near * 384 + 384)
        part = (tn_dot(high[:, lanes], left[near]) + tn_dot(low[:, lanes], left[near]))[:320]
        total[...] = part if near == 0 else total[...] + part


def on_device(tokens, base_weight, left_factors, right_factors, member_of, ranks):
    z, xl, core, y, xh = (lax.axis_index(name) for name in AXES)
    members = M_DEV * 64
    left = left_factors.astype(BF16).reshape(32, IN_BLOCK)
    tensor = y * 2 + xh
    place = jnp.stack([z, core, xl ^ xh, y, xh, xl, tensor]).astype(jnp.int32)
    slot = jnp.concatenate([move(base_weight.T.astype(BF16), half_target), left])
    slots = lax.all_gather(slot, "z", axis=0, tiled=True)

    levels = rank_row(ranks)
    chunk = spread_right(right_factors, levels, z, tensor)
    other = move(after(jnp.concatenate([tokens, left]), chunk), xh_target)
    rows = jnp.concatenate([tokens, other[:ROWS]])
    rows = jnp.concatenate([rows, move(rows, xl_target)])
    rows = jnp.concatenate([rows, move(rows, core_target)])
    right = gather_right(chunk)
    keep, give = call(
        functools.partial(update_kernel, members),
        (shape(160, IN_BLOCK), shape(160, IN_BLOCK)),
        place,
        (slots, right),
        [
            pltpu.VMEM((320, IN_BLOCK), F32),
            pltpu.VMEM((2, 256, IN_BLOCK), BF16),
            pltpu.VMEM((256, GROUP_ROWS), BF16),
            pltpu.VMEM((256, GROUP_ROWS), BF16),
        ],
        flops=8 * 384 * 256 * 640,
    )
    keep, give = call(
        join_kernel,
        (shape(OUT_BLOCK, IN_BLOCK), shape(OUT_BLOCK, IN_BLOCK)),
        place,
        (keep, move(give, core_target)),
    )
    update = keep + move(give, xl_target)

    (give,) = call(
        product_kernel,
        (shape(4, GIVE, GROUP_ROWS, dtype=BF16),),
        place + zero_after(right),
        (slots, rows, left, other[ROWS:], member_of),
        [pltpu.VMEM((2, IN_BLOCK, IN_BLOCK), BF16), pltpu.VMEM((2, GROUP_ROWS, IN_BLOCK), BF16)],
        flops=2 * 768 * 640 * 1280,
        moved=6 * 2**20,
    )
    got = lax.all_to_all(give, "y", split_axis=0, concat_axis=0, tiled=True)
    block = (160, 256)
    mine, coefficient, to_core, to_xl, to_diagonal = call(
        sum_kernel,
        (shape(*block), shape(8, ROWS), shape(*block))
        + (shape(*block, dtype=BF16), shape(*block, dtype=BF16)),
        place,
        (got,),
    )
    right_local = lax.dynamic_slice_in_dim(right_factors, tensor * IN_BLOCK, IN_BLOCK, 2)
    (outputs,) = call(
        functools.partial(finish_kernel, perturb_scale / math.sqrt(RANK)),
        (shape(ROWS, IN_BLOCK),),
        place,
        (
            mine,
            move(to_core, core_target),
            move(to_xl, xl_target),
            move(to_diagonal, diagonal_target),
            coefficient,
            right_local.reshape(32, IN_BLOCK),
            member_of,
        ),
        [pltpu.VMEM((IN_BLOCK, 256), F32)],
        flops=12 * ROWS * 32 * IN_BLOCK,
    )
    return (outputs, update.T)


def solution(mesh):
    fine = Mesh(mesh.devices.reshape(tuple(SIZES.values())), AXES)
    return jax.shard_map(
        on_device,
        mesh=fine,
        in_specs=(
            P(POP, TENSOR),
            P(TENSOR, POP),
            P(POP, None, TENSOR),
            P(POP, None, None),
            P(POP, None),
            P(POP),
        ),
        out_specs=(P(POP, TENSOR), P(TENSOR, POP)),
        check_vma=False,
    )
```
